32 devices in a mesh: dp: 4 (over x, core), tensor: 8 (over z, y).
Axes of the slice: x: 2, y: 2, z: 4, core: 2. Of those that a mesh axis runs over, the one named last changes fastest.
Arguments:
- inputs: bfloat16 [8192, 1024], P(('dp', 'tensor')), may hold values from -6 to 6
- segments: int32 [8, 1024], P('dp'), may hold values from 0 to 7, never falling along the last dimension, each value on 1 to 512 neighbouring positions
- query_weight: bfloat16 [2, 1024, 1024], P(None, None, 'tensor'), may hold values from -0.1875 to 0.1875
- query_bias: float32 [2, 1024], P(None, 'tensor'), may hold values from -1.2 to 1.2
- key_weight: bfloat16 [2, 1024, 1024], P(None, None, 'tensor'), may hold values from -0.1875 to 0.1875
- value_weight: bfloat16 [2, 1024, 1024], P(None, None, 'tensor'), may hold values from -0.1875 to 0.1875
- value_bias: float32 [2, 1024], P(None, 'tensor'), may hold values from -1.2 to 1.2
- out_weight: bfloat16 [2, 1024, 1024], P(None, 'tensor'), may hold values from -0.75 to 0.75
- out_bias: float32 [2, 1024], replicated, may hold values from -1.2 to 1.2
- first_gain: float32 [2, 1024], replicated, may hold values from 0.5 to 1.5
- first_shift: float32 [2, 1024], replicated, may hold values from -1.2 to 1.2
- inner_weight: bfloat16 [2, 1024, 4096], P(None, None, 'tensor'), may hold values from -0.1875 to 0.1875
- inner_bias: float32 [2, 4096], P(None, 'tensor'), may hold values from -1.2 to 1.2
- outer_weight: bfloat16 [2, 4096, 1024], P(None, 'tensor'), may hold values from -0.125 to 0.125
- outer_bias: float32 [2, 1024], replicated, may hold values from -1.2 to 1.2
- second_gain: float32 [2, 1024], replicated, may hold values from 0.5 to 1.5
- second_shift: float32 [2, 1024], replicated, may hold values from -1.2 to 1.2
- cotangent: bfloat16 [8192, 1024], P(('dp', 'tensor')), may hold values from -6 to 6
Outputs:
- result: float32 [8192, 1024], P(('dp', 'tensor'))
- input_grad: float32 [8192, 1024], P(('dp', 'tensor'))
- grad_query_weight: float32 [2, 1024, 1024], P(None, None, 'tensor')
- grad_query_bias: float32 [2, 1024], P(None, 'tensor')
- grad_key_weight: float32 [2, 1024, 1024], P(None, None, 'tensor')
- grad_value_weight: float32 [2, 1024, 1024], P(None, None, 'tensor')
- grad_value_bias: float32 [2, 1024], P(None, 'tensor')
- grad_out_weight: float32 [2, 1024, 1024], P(None, 'tensor')
- grad_out_bias: float32 [2, 1024], replicated
- grad_first_gain: float32 [2, 1024], replicated
- grad_first_shift: float32 [2, 1024], replicated
- grad_inner_weight: float32 [2, 1024, 4096], P(None, None, 'tensor')
- grad_inner_bias: float32 [2, 4096], P(None, 'tensor')
- grad_outer_weight: float32 [2, 4096, 1024], P(None, 'tensor')
- grad_outer_bias: float32 [2, 1024], replicated
- grad_second_gain: float32 [2, 1024], replicated
- grad_second_shift: float32 [2, 1024], replicated
The draws below stay inside these ranges and needn't reach their ends.
Inputs may be any that keep to these rules, and one draw needn't show every extreme that they name: `segments`: within each sequence segment numbers never fall; a document holds 1 to 512 tokens, and some document holds exactly 512.
All inputs are finite; a program needn't handle non-finite values.
Results may differ from the reference program's by a relative error of at most 0.04.
Values may be sent and summed in bfloat16 or wider, within the bound.
No kernel may reach another device: no remote copies, remote signals or barrier semaphores. Data moves between devices by JAX's collectives and lax.ppermute only.
A program may use at most 192 MiB of HBM per device.

```python
import math
from functools import partial
import jax
import jax.numpy as jnp
import numpy as np
from jax import lax

D = 1024
FF = 4096
HD = 64
LAYERS = 2
L = 1024
WINDOW = 256
DOCS = 8
SEQS = 8
TOKENS = 8192


def level_of(own_key, dims, pieces, smallest, high):
    def one(dim, shards_of):
        steps = jax.random.uniform(jax.random.fold_in(jax.random.fold_in(own_key, 6), dim), (shards_of,), jnp.float32, smallest / len(pieces), high / len(pieces))
        return jnp.repeat(jnp.exp(steps), dims[dim] // shards_of).reshape((-1,) + (1,) * (len(dims) - dim - 1))

    factor_of = one(*pieces[0])
    for cut in pieces[1:]:
        factor_of = factor_of * one(*cut)
    return factor_of


def split_up(number_of, total, reach, lean):
    loads = [(1 << 20) // math.isqrt(rank ** lean) + 1 for rank in range(2, number_of + 1)]
    surplus, given = total - reach - (number_of - 1), [1] * (number_of - 1)
    while surplus > 0:
        free = [i for i in range(number_of - 1) if given[i] < reach]
        pool, left = sum([loads[i] for i in free]), surplus
        for i in free:
            extra = min(reach - given[i], max(1, left * loads[i] // pool), surplus)
            given[i] = given[i] + extra
            surplus = surplus - extra
    return np.array([reach] + given)


def ragged_sizes(key, number_of, total, bound, lean):
    if number_of == 2:
        one = jax.random.randint(key, (), max(1, total - bound), min(bound, total - 1) + 1)
        return jnp.stack([one, total - one])
    lengths = jnp.asarray(split_up(number_of, total, bound, lean), jnp.int32)
    pairs = (number_of - 1) // 2
    giver, sink = lengths[1:1 + 2 * pairs:2], lengths[2:2 + 2 * pairs:2]
    room = jnp.minimum(giver - 1, bound - sink)
    passed = jax.random.randint(jax.random.fold_in(key, 1), (pairs,), 0, 1 << 20) % (room + 1)
    lengths = lengths.at[1:1 + 2 * pairs:2].set(giver - passed).at[2:2 + 2 * pairs:2].set(sink + passed)
    return lengths[jax.random.permutation(jax.random.fold_in(key, 2), number_of)]


def gaussian(key, extent, scale, bound, pieces=(), kind=jnp.bfloat16):
    values = jax.random.normal(key, extent, jnp.float32) * scale
    if len(pieces) > 0:
        values = level_of(key, extent, pieces, -0.22, 0.18) * values
    return jnp.clip(values, min=-bound, max=bound).astype(kind)


def setup_inputs(seed: int = 0) -> dict:
    splits = jax.random.split(jax.random.key(seed), 19)
    return {
        "inputs": gaussian(splits[0], (TOKENS, D), 1.0, 6.0, ((0, 32),)),
        "segments": jax.vmap(lambda own: jnp.searchsorted(jnp.cumsum(ragged_sizes(own, DOCS, L, L // 2, 2)), jnp.arange(L), side="right"))(jax.random.split(splits[1], SEQS)).reshape((SEQS, L)).astype(jnp.int32),
        "query_weight": gaussian(splits[2], (LAYERS, D, D), D ** -0.5, 0.1875, ((2, 8),)),
        "query_bias": gaussian(splits[3], (LAYERS, D), 0.2, 1.2, ((1, 8),), jnp.float32),
        "key_weight": gaussian(splits[4], (LAYERS, D, D), D ** -0.5, 0.1875, ((2, 8),)),
        "value_weight": gaussian(splits[5], (LAYERS, D, D), D ** -0.5, 0.1875, ((2, 8),)),
        "value_bias": gaussian(splits[6], (LAYERS, D), 0.2, 1.2, ((1, 8),), jnp.float32),
        "out_weight": gaussian(splits[7], (LAYERS, D, D), (D // 16) ** -0.5, 0.75, ((1, 8),)),
        "out_bias": gaussian(splits[8], (LAYERS, D), 0.2, 1.2, (), jnp.float32),
        "first_gain": jnp.clip(1.0 + 0.1 * jax.random.normal(splits[9], (LAYERS, D), jnp.float32), 0.5, 1.5),
        "first_shift": gaussian(splits[10], (LAYERS, D), 0.2, 1.2, (), jnp.float32),
        "inner_weight": gaussian(splits[11], (LAYERS, D, FF), D ** -0.5, 0.1875, ((2, 8),)),
        "inner_bias": gaussian(splits[12], (LAYERS, FF), 0.2, 1.2, ((1, 8),), jnp.float32),
        "outer_weight": gaussian(splits[13], (LAYERS, FF, D), (FF // 2) ** -0.5, 0.125, ((1, 8),)),
        "outer_bias": gaussian(splits[14], (LAYERS, D), 0.2, 1.2, (), jnp.float32),
        "second_gain": jnp.clip(1.0 + 0.1 * jax.random.normal(splits[15], (LAYERS, D), jnp.float32), 0.5, 1.5),
        "second_shift": gaussian(splits[16], (LAYERS, D), 0.2, 1.2, (), jnp.float32),
        "cotangent": gaussian(splits[17], (TOKENS, D), 1.0, 6.0, ((0, 32),)),
    }


@jax.custom_vjp
def low(v):
    return lax.optimization_barrier(v.astype(jnp.bfloat16)).astype(jnp.float32)

@jax.custom_vjp
def low_back(v):
    return v

def low_keep(v):
    return (low(v), None)

def low_pass(kept, grad):
    return (grad,)

def back_keep(v):
    return (v, None)

def back_low(kept, grad):
    return (low(grad),)
low.defvjp(low_keep, low_pass)
low_back.defvjp(back_keep, back_low)
EPS = 1e-05
NEGATIVE = -1e+30
HIGHEST = lax.Precision.HIGHEST

def matmul(left, right):
    return jnp.dot(left, right, precision=HIGHEST, preferred_element_type=jnp.float32)

def layer_norm(values, norm_gain, norm_shift):
    center = values - lax.optimization_barrier(jnp.mean(values, axis=-1, keepdims=True))
    spread = lax.optimization_barrier(jnp.mean(center * center, axis=-1, keepdims=True))
    return center * lax.rsqrt(spread + EPS) * norm_gain + norm_shift

def key_mask(seg_row, windowed):
    allowed = seg_row[:, None] == seg_row[None, :]
    if windowed:
        places = jnp.arange(seg_row.shape[0], dtype=jnp.int32)
        in_window = jnp.abs(places[:, None] - places[None, :]) <= WINDOW // 2
        allowed = jnp.logical_and(allowed, in_window)
    return allowed

def attend_sequence(blocks, windowed):
    query_rows, key_rows, value_rows, seg_row = blocks
    score_scale = query_rows.shape[-1] ** (-0.5)
    scores = low_back(jnp.einsum('qhd,khd->hqk', query_rows, key_rows, precision=HIGHEST) * score_scale)
    allowed = key_mask(seg_row, windowed)
    attn_probs = jax.nn.softmax(jnp.where(allowed[None], scores, NEGATIVE), axis=-1)
    return jnp.einsum('hqk,khd->qhd', low(attn_probs), value_rows, precision=HIGHEST)

def encoder_layer(hidden_in, weights, windowed, segments):
    query_weight, query_bias, key_weight, value_weight, value_bias, out_weight, out_bias, first_gain, first_shift, inner_weight, inner_bias, outer_weight, outer_bias, second_gain, second_shift = weights
    rows_low = low(hidden_in)
    query_all = low_back(low(matmul(rows_low, query_weight) + query_bias))
    key_all = low_back(low(matmul(rows_low, key_weight)))
    value_all = low_back(low(matmul(rows_low, value_weight) + value_bias))
    seq_count, length = segments.shape
    head_count = query_weight.shape[1] // HD

    def shaped(array):
        return array.reshape(seq_count, length, head_count, HD)
    context = lax.map(jax.checkpoint(partial(attend_sequence, windowed=windowed)), (shaped(query_all), shaped(key_all), shaped(value_all), segments))
    context = low_back(low(context.reshape(hidden_in.shape[0], -1)))
    attended = hidden_in + low_back(matmul(context, out_weight)) + out_bias
    normed = layer_norm(attended, first_gain, first_shift)
    inner = low_back(matmul(low(normed), inner_weight) + inner_bias)
    activated = low(jax.nn.gelu(inner, approximate=False))
    mixed = normed + low_back(matmul(activated, outer_weight)) + outer_bias
    return layer_norm(mixed, second_gain, second_shift)

def reference(inputs, segments, query_weight, query_bias, key_weight, value_weight, value_bias, out_weight, out_bias, first_gain, first_shift, inner_weight, inner_bias, outer_weight, outer_bias, second_gain, second_shift, cotangent):
    weights = tuple((array.astype(jnp.float32) for array in (query_weight, query_bias, key_weight, value_weight, value_bias, out_weight, out_bias, first_gain, first_shift, inner_weight, inner_bias, outer_weight, outer_bias, second_gain, second_shift)))

    def forward(hidden_in, *params):
        for layer_index in range(LAYERS):
            layer_weights = tuple((array[layer_index] for array in params))
            hidden_in = encoder_layer(hidden_in, layer_weights, layer_index % 2 == 1, segments)
        return hidden_in
    result, backward = jax.vjp(forward, inputs.astype(jnp.float32), *weights)
    grads = backward(cotangent.astype(jnp.float32))
    return (result, grads[0], grads[1], grads[2], grads[3], grads[4], grads[5], grads[6], grads[7], grads[8], grads[9], grads[10], grads[11], grads[12], grads[13], grads[14], grads[15])
```

```python
from functools import partial

import jax
import jax.numpy as jnp
from jax import lax
from jax.experimental import pallas as pl
from jax.experimental.pallas import tpu as pltpu
from jax.sharding import PartitionSpec as P

HD = 64
WINDOW = 256
EPS = 1e-05
NEGATIVE = -1e30
BF = jnp.bfloat16
F32 = jnp.float32
LANES = 128


def dot_nn(left, right):
    return lax.dot_general(left, right, (((1,), (0,)), ((), ())), preferred_element_type=F32)


def dot_nt(left, right):
    return lax.dot_general(left, right, (((1,), (1,)), ((), ())), preferred_element_type=F32)


def dot_tn(left, right):
    return lax.dot_general(left, right, (((0,), (0,)), ((), ())), preferred_element_type=F32)


def allowed_keys(seg_q, seg_k, halo):
    allowed = seg_q == seg_k
    if halo:
        row = lax.broadcasted_iota(jnp.int32, allowed.shape, 0)
        col = lax.broadcasted_iota(jnp.int32, allowed.shape, 1)
        allowed = jnp.logical_and(allowed, jnp.abs(row + halo - col) <= WINDOW // 2)
    return allowed


def head_lanes(shape, head):
    lane = lax.broadcasted_iota(jnp.int32, shape, 1)
    return (lane // HD) == head


def probabilities(query, key, allowed):
    scores = jnp.where(allowed, dot_nt(query, key) * (HD ** -0.5), NEGATIVE)
    raised = jnp.exp(scores - jnp.max(scores, axis=-1, keepdims=True))
    return raised * (1.0 / jnp.sum(raised, axis=-1, keepdims=True))


def attend_kernel(halo, seg_q_ref, seg_k_ref, q_ref, k_ref, v_ref, c_ref):
    allowed = allowed_keys(seg_q_ref[...], seg_k_ref[...], halo)
    query, key, value = q_ref[...], k_ref[...], v_ref[...]
    total = None
    for head in range(LANES // HD):
        mine = head_lanes(query.shape, head)
        probs = probabilities(jnp.where(mine, query, jnp.zeros_like(query)), key, allowed)
        part = jnp.where(mine, dot_nn(probs.astype(BF), value), 0.0)
        total = part if total is None else total + part
    c_ref[...] = total.astype(BF)


def attend_back_kernel(halo, seg_q_ref, seg_k_ref, q_ref, k_ref, v_ref, g_ref, dq_ref, dk_ref, dv_ref):
    allowed = allowed_keys(seg_q_ref[...], seg_k_ref[...], halo)
    query, key, value, grad = q_ref[...], k_ref[...], v_ref[...], g_ref[...]
    dq = dk = dv = None
    for head in range(LANES // HD):
        mine = head_lanes(query.shape, head)
        own_q = jnp.where(mine, query, jnp.zeros_like(query))
        own_g = jnp.where(mine, grad, jnp.zeros_like(grad))
        probs = probabilities(own_q, key, allowed)
        grad_probs = dot_nt(own_g, value)
        delta = jnp.sum(probs * grad_probs, axis=-1, keepdims=True)
        grad_scores = (probs * (grad_probs - delta)).astype(BF)
        q_part = jnp.where(mine, dot_nn(grad_scores, key), 0.0)
        k_part = dot_tn(grad_scores, own_q)
        v_part = dot_tn(probs.astype(BF), own_g)
        dq = q_part if dq is None else dq + q_part
        dk = k_part if dk is None else dk + k_part
        dv = v_part if dv is None else dv + v_part
    dq_ref[...] = (dq * (HD ** -0.5)).astype(BF)
    dk_ref[...] = (dk * (HD ** -0.5)).astype(BF)
    dv_ref[...] = dv.astype(BF)


def attend(query, key, value, seg_q, seg_k, halo):
    rows, width = query.shape
    keys = key.shape[0]
    whole = lambda shape: pl.BlockSpec(shape, lambda p: (0, 0))
    near = pl.BlockSpec((rows, LANES), lambda p: (0, p))
    far = pl.BlockSpec((keys, LANES), lambda p: (0, p))
    return pl.pallas_call(
        partial(attend_kernel, halo),
        grid=(width // LANES,),
        in_specs=[whole((rows, 1)), whole((1, keys)), near, far, far],
        out_specs=near,
        out_shape=jax.ShapeDtypeStruct((rows, width), BF),
        compiler_params=pltpu.CompilerParams(vmem_limit_bytes=40 * 1024 * 1024),
        cost_estimate=pl.CostEstimate(flops=HINT, bytes_accessed=HINT, transcendentals=0),
        name="attend",
    )(seg_q, seg_k, query, key, value)


def attend_back(query, key, value, grad, seg_q, seg_k, halo):
    rows, width = query.shape
    keys = key.shape[0]
    whole = lambda shape: pl.BlockSpec(shape, lambda p: (0, 0))
    near = pl.BlockSpec((rows, LANES), lambda p: (0, p))
    far = pl.BlockSpec((keys, LANES), lambda p: (0, p))
    return pl.pallas_call(
        partial(attend_back_kernel, halo),
        grid=(width // LANES,),
        in_specs=[whole((rows, 1)), whole((1, keys)), near, far, far, near],
        out_specs=[near, far, far],
        out_shape=[
            jax.ShapeDtypeStruct((rows, width), BF),
            jax.ShapeDtypeStruct((keys, width), BF),
            jax.ShapeDtypeStruct((keys, width), BF),
        ],
        compiler_params=pltpu.CompilerParams(vmem_limit_bytes=48 * 1024 * 1024),
        cost_estimate=pl.CostEstimate(flops=HINT, bytes_accessed=HINT, transcendentals=0),
        name="attend_back",
    )(seg_q, seg_k, query, key, value, grad)


def norm_stats(values):
    center = values - jnp.mean(values, axis=-1, keepdims=True)
    inverse = lax.rsqrt(jnp.mean(center * center, axis=-1, keepdims=True) + EPS)
    return center * inverse, inverse


def norm_back(grad, normal, inverse, gain):
    scaled = grad * gain
    back = inverse * (
        scaled
        - jnp.mean(scaled, axis=-1, keepdims=True)
        - normal * jnp.mean(scaled * normal, axis=-1, keepdims=True)
    )
    return back, jnp.sum(grad * normal, axis=0), jnp.sum(grad, axis=0)


def gelu_and_slope(inner):
    half = 0.5 * (1.0 + lax.erf(inner * (0.5 ** 0.5)))
    bell = jnp.exp(-0.5 * inner * inner) * ((2.0 * jnp.pi) ** -0.5)
    return (inner * half).astype(BF), (half + inner * bell).astype(BF)


def streamed(kernel_step, near, first, second, extra, outs, name):
    count, (rows_of, width) = len(first), first[0].shape
    tile = min(512, rows_of)
    steps = [(k, t * tile) for k in range(count) for t in range(rows_of // tile)]
    near_count, extra_count = len(near), len(extra)

    def kernel(*refs):
        near_refs, refs = refs[:near_count], refs[near_count:]
        extra_refs, refs = refs[:extra_count], refs[extra_count:]
        one_refs, two_refs, refs = refs[:count], refs[count : 2 * count], refs[2 * count :]
        *out_refs, one_held, two_held, sems = refs

        def copies(s):
            k, at = steps[s]
            slot = s % 2
            return [
                pltpu.make_async_copy(one_refs[k].at[pl.ds(at, tile)], one_held.at[slot], sems.at[0, slot]),
                pltpu.make_async_copy(two_refs[k].at[pl.ds(at, tile)], two_held.at[slot], sems.at[1, slot]),
            ]

        for copy in copies(0):
            copy.start()
        for s, (k, at) in enumerate(steps):
            if s + 1 < len(steps):
                for copy in copies(s + 1):
                    copy.start()
            for copy in copies(s):
                copy.wait()
            kernel_step(s, k, at, tile, near_refs, extra_refs, one_held.at[s % 2], two_held.at[s % 2], out_refs)

    whole = pl.BlockSpec(memory_space=pltpu.VMEM)
    anywhere = pl.BlockSpec(memory_space=pl.ANY)
    dtype = first[0].dtype
    return pl.pallas_call(
        kernel,
        in_specs=[whole] * (near_count + extra_count) + [anywhere] * (2 * count),
        out_specs=[whole] * len(outs),
        out_shape=outs,
        scratch_shapes=[
            pltpu.VMEM((2, tile, width), dtype),
            pltpu.VMEM((2, tile, width), dtype),
            pltpu.SemaphoreType.DMA((2, 2)),
        ],
        compiler_params=pltpu.CompilerParams(vmem_limit_bytes=40 * 1024 * 1024),
        cost_estimate=pl.CostEstimate(flops=HINT, bytes_accessed=HINT, transcendentals=0),
        name=name,
    )(*near, *extra, *first, *second)


def feed_forward(rows_low, inner, outer, bias):
    count, (each, width), rows = len(inner), inner[0].shape, rows_low.shape[0]

    def step(s, k, at, tile, near, extra, inner_tile, outer_tile, outs):
        act, slope = gelu_and_slope(
            dot_nt(near[0][...], inner_tile[...]) + extra[0][pl.ds(k, 1), pl.ds(at, tile)]
        )
        outs[1 + k][:, pl.ds(at, tile)] = act
        outs[1 + count + k][:, pl.ds(at, tile)] = slope
        part = dot_nn(act, outer_tile[...])
        outs[0][...] = part if s == 0 else outs[0][...] + part

    shapes = [jax.ShapeDtypeStruct((rows, width), F32)] + [jax.ShapeDtypeStruct((rows, each), BF)] * (2 * count)
    total, *rest = streamed(step, [rows_low], inner, outer, [bias], shapes, "feed_forward")
    return total, rest[:count], rest[count:]


def feed_forward_back(grad_low, inner, outer, slopes):
    count, (each, width), rows = len(inner), inner[0].shape, grad_low.shape[0]

    def step(s, k, at, tile, near, extra, outer_tile, inner_tile, outs):
        grad = (dot_nt(near[0][...], outer_tile[...]) * extra[k][:, pl.ds(at, tile)].astype(F32)).astype(BF)
        outs[2 + k][:, pl.ds(at, tile)] = grad
        outs[1][pl.ds(k, 1), pl.ds(at, tile)] = jnp.sum(grad.astype(F32), axis=0, keepdims=True)
        part = dot_nn(grad, inner_tile[...])
        outs[0][...] = part if s == 0 else outs[0][...] + part

    shapes = [jax.ShapeDtypeStruct((rows, width), F32), jax.ShapeDtypeStruct((count, each), F32)]
    shapes += [jax.ShapeDtypeStruct((rows, each), BF)] * count
    total, sums, *grads = streamed(step, [grad_low], outer, inner, list(slopes), shapes, "feed_forward_back")
    return total, sums, grads


def weight_grad(pairs, add=None):
    columns, width = pairs[0][0].shape[1], pairs[0][1].shape[1]
    tile = min(256, columns)

    def kernel(*refs):
        total = None
        for k in range(len(pairs)):
            part = dot_tn(refs[2 * k][...], refs[2 * k + 1][...])
            total = part if total is None else total + part
        if add is not None:
            total = total + refs[2 * len(pairs)][...].astype(F32)
        refs[-1][...] = total.astype(BF)

    block = pl.BlockSpec((tile, width), lambda t: (t, 0))
    specs, operands = [], []
    for left, right in pairs:
        specs += [
            pl.BlockSpec((left.shape[0], tile), lambda t: (0, t)),
            pl.BlockSpec(right.shape, lambda t: (0, 0)),
        ]
        operands += [left, right]
    if add is not None:
        specs.append(block)
        operands.append(add)
    return pl.pallas_call(
        kernel,
        grid=(columns // tile,),
        in_specs=specs,
        out_specs=block,
        out_shape=jax.ShapeDtypeStruct((columns, width), BF),
        compiler_params=pltpu.CompilerParams(vmem_limit_bytes=32 * 1024 * 1024),
        cost_estimate=pl.CostEstimate(flops=HINT, bytes_accessed=HINT, transcendentals=0),
        name="weight_grad",
    )(*operands)


def gradients_out(turned, plain):
    layers, width = len(turned[0]), turned[0][0].shape[1]
    steps = 4

    def kernel(*refs):
        outs = refs[layers * (len(turned) + len(plain)) :]
        for k, out in enumerate(outs):
            for l in range(layers):
                value = refs[k * layers + l][...].astype(F32)
                out[l] = value.T if k < len(turned) else value

    specs, shapes, out_specs = [], [], []
    for arrays in turned:
        rows = arrays[0].shape[0]
        specs += [pl.BlockSpec((rows, width // steps), lambda t: (0, t))] * layers
        out_specs.append(pl.BlockSpec((layers, width // steps, rows), lambda t: (0, t, 0)))
        shapes.append(jax.ShapeDtypeStruct((layers, width, rows), F32))
    for arrays in plain:
        rows = arrays[0].shape[0]
        specs += [pl.BlockSpec((rows // steps, width), lambda t: (t, 0))] * layers
        out_specs.append(pl.BlockSpec((layers, rows // steps, width), lambda t: (0, t, 0)))
        shapes.append(jax.ShapeDtypeStruct((layers, rows, width), F32))
    return pl.pallas_call(
        kernel,
        grid=(steps,),
        in_specs=specs,
        out_specs=out_specs,
        out_shape=shapes,
        compiler_params=pltpu.CompilerParams(vmem_limit_bytes=40 * 1024 * 1024),
        cost_estimate=pl.CostEstimate(flops=HINT, bytes_accessed=HINT, transcendentals=0),
        name="gradients_out",
    )(*[a for arrays in turned + plain for a in arrays])


class Grid:
    def __init__(self, mesh):
        self.nd, self.nt = mesh.shape["dp"], mesh.shape["tensor"]
        self.nx = self.nd // 2

    def place(self):
        self.dp, self.tensor = lax.axis_index("dp"), lax.axis_index("tensor")
        self.x, self.c = self.dp // 2, self.dp % 2

    def swap(self, array, axis, bit):
        count = self.nd if axis == "dp" else self.nt
        return lax.ppermute(array, axis, [(i, i ^ bit) for i in range(count)])

    def core(self, array):
        return self.swap(array, "dp", 1)

    def bits(self, name):
        low, high = {"x": (2, self.nd), "t": (1, self.nt)}[name]
        found = []
        while low < high:
            found.append(low)
            low *= 2
        return found

    def shift(self, array, by, group):
        pairs = [(i, i + by) for i in range(self.nt) if 0 <= i + by < self.nt and i // group == (i + by) // group]
        return lax.ppermute(array, "tensor", pairs)

    def turned(self, array, name, axis):
        count, at = {"x": (self.nx, self.x), "c": (2, self.c), "t": (self.nt, self.tensor)}[name]
        if count == 2:
            return jnp.where(at == 0, array, lax.rev(array, (axis,)))
        return jnp.take(array, at ^ jnp.arange(count), axis=axis)

    def sum_all(self, array):
        for axis, count in (("dp", self.nd), ("tensor", self.nt)):
            bit = 1
            while bit < count:
                array = array + self.swap(array, axis, bit)
                bit *= 2
        return array


def together(*values):
    return lax.optimization_barrier(values)


def shards(
    grid,
    inputs,
    segments,
    query_weight,
    query_bias,
    key_weight,
    value_weight,
    value_bias,
    out_weight,
    out_bias,
    first_gain,
    first_shift,
    inner_weight,
    inner_bias,
    outer_weight,
    outer_bias,
    second_gain,
    second_shift,
    cotangent,
):
    g = grid
    g.place()
    layers = query_weight.shape[0]
    rows, width = inputs.shape
    heads = query_weight.shape[2]
    cores = 2 if heads // 2 % HD == 0 else 1
    part = heads // cores
    units = inner_weight.shape[2]
    block = units // g.nd
    length = segments.shape[1]
    group = length // rows
    halo = WINDOW // 2
    high_to_low = g.bits("t")[::-1]

    own = segments[g.tensor // group] if segments.shape[0] > 1 else segments[0]
    spot = g.tensor % group
    seg_q = lax.dynamic_slice(own, (spot * rows,), (rows,))[:, None]
    padded = jnp.pad(own, (halo, halo), constant_values=-1)
    seg_near = lax.dynamic_slice(padded, (spot * rows,), (rows + 2 * halo,))[None]
    seg_far = jnp.take(own.reshape(group, rows), spot ^ jnp.arange(group), axis=0).reshape(1, length)

    def far_rows(array, other=None):
        bit = 1
        while bit < group:
            if other is None:
                other = g.swap(array, "tensor", bit)
            array, other = jnp.concatenate([array, other]), None
            bit *= 2
        return array

    def far_sums(array):
        bit = group // 2
        while bit:
            keep, give = jnp.split(array, 2)
            array = keep.astype(F32) + g.swap(give.astype(BF), "tensor", bit).astype(F32)
            bit //= 2
        return array

    def near_rows(array):
        return jnp.concatenate(
            [g.shift(array[rows - halo :], 1, group), array, g.shift(array[:halo], -1, group)]
        )

    def near_sums(array):
        after_rows = g.shift(array[:halo], -1, group).astype(F32)
        before_rows = g.shift(array[rows + halo :], 1, group).astype(F32)
        edge = jnp.zeros((rows - halo, width), F32)
        return (
            array[halo : rows + halo].astype(F32)
            + jnp.concatenate([edge, after_rows])
            + jnp.concatenate([before_rows, edge])
        )

    step_order = [0]
    for bit in high_to_low:
        step_order = step_order + [m | bit for m in step_order]
    blocks = 2 * g.nx

    def by_steps(array):
        for bit in high_to_low:
            array = jnp.concatenate([array, g.swap(array, "tensor", bit)])
        return array

    def back_by_steps(total):
        for bit in high_to_low[::-1]:
            keep, give = jnp.split(total, 2)
            total = (keep.astype(F32) + g.swap(give, "tensor", bit).astype(F32)).astype(BF)
        return total

    def from_steps(array, axis):
        place = jnp.array([step_order.index(m) for m in range(g.nt)])
        return jnp.take(array, place[g.tensor ^ jnp.arange(g.nt)], axis=axis)

    def unit_piece(shard):
        return lax.dynamic_index_in_dim(shard.reshape(g.nd, block, width), g.dp, 0, keepdims=False)

    def over_x(array):
        pieces = [array]
        for bit in g.bits("x"):
            pieces = pieces + [g.swap(a, "dp", bit) for a in pieces]
        return pieces

    def over_core(pieces):
        return pieces + [g.core(a) for a in pieces]

    def head_piece(l):
        pack = jnp.stack([query_weight[l].T, key_weight[l].T, value_weight[l].T, out_weight[l]])
        if cores == 2:
            pack = lax.dynamic_index_in_dim(pack.reshape(4, 2, part, width), g.c, 1, keepdims=False)
        return pack.reshape(1, 4 * part, width)

    def head_first(pack):
        for bit in high_to_low[:-1]:
            pack = jnp.concatenate([pack, g.swap(pack, "tensor", bit)])
        return pack

    def head_last(pack):
        both = [pack, g.swap(pack, "tensor", high_to_low[-1])]
        return [
            jnp.concatenate([a[:, k * part : (k + 1) * part].reshape(-1, width) for a in both]) for k in range(4)
        ]

    def head_rows(kinds):
        return [[a] if cores == 1 else [a, g.core(a)] for a in kinds]

    def bias_rows():
        pack = by_steps(jnp.concatenate([inner_bias, query_bias, value_bias], axis=1)[None])
        unit = pack[..., :units].reshape(g.nt, layers, g.nx, 2, block)
        unit = g.turned(g.turned(unit, "x", 2), "c", 3)
        head = pack[..., units:].reshape(g.nt, layers, 2, cores, part)
        if cores == 2:
            head = g.turned(head, "c", 3)
        unit = jnp.concatenate([unit[:, :1], from_steps(unit[:, 1:], 0)], 1)
        head = jnp.concatenate([head[:, :1], from_steps(head[:, 1:], 0)], 1)
        unit = jnp.transpose(unit, (1, 3, 2, 0, 4)).reshape(layers, blocks, -1)
        return unit, jnp.transpose(head, (1, 2, 3, 0, 4)).reshape(layers, 2, cores, -1)

    moves = [(l, kind) for l in range(layers) for kind in "iu"]
    shard_of = {(l, kind): {"i": inner_weight[l].T, "u": outer_weight[l]}[kind] for l, kind in moves}
    piece_of, gathered, spread, unit_w, head_w = {}, {}, {}, {}, {}
    piece_of[moves[0]] = unit_piece(shard_of[moves[0]])
    stage = 0

    def next_round():
        nonlocal stage
        new = {"piece_of": {}, "gathered": {}, "spread": {}, "unit_w": {}}
        for back, name in enumerate(new):
            if 0 <= stage + 1 - back < len(moves):
                key = moves[stage + 1 - back]
                if back > 1 or key[0] == 0:
                    new[name][key] = (
                        unit_piece(shard_of[key]) if back == 0
                        else by_steps(piece_of[key]) if back == 1
                        else over_x(gathered[key]) if back == 2
                        else over_core(spread[key])
                    )
        stage += 1
        return new

    def end_round(new, carry):
        new, carry = together(new, carry)
        for name, kept in (("piece_of", piece_of), ("gathered", gathered), ("spread", spread), ("unit_w", unit_w)):
            kept.update(new[name])
        return carry

    saved = []
    hidden = inputs.astype(F32)
    for l in range(1, layers):
        pieces = jnp.stack([unit_piece(shard_of[l, "i"]), unit_piece(shard_of[l, "u"])])
        both = lax.all_gather(pieces, "tensor", axis=0)
        for k, kind in enumerate("iu"):
            gathered[l, kind] = both[:, k].reshape(-1, width)
    new = next_round()
    unit_bias, head_bias = bias_rows()
    far = g.swap(inputs, "tensor", 1) if group > 1 else inputs
    first_part = head_first(head_piece(0))
    unit_bias, head_bias, far, first_part = end_round(new, (unit_bias, head_bias, far, first_part))
    new = next_round()
    far_inputs = far_rows(inputs, far)
    kinds = head_last(first_part)
    later = [head_piece(l).reshape(4, part, width) for l in range(1, layers)]
    hidden, far_inputs, kinds, later = end_round(new, (hidden, far_inputs, kinds, later))
    for l in range(layers):
        windowed = l % 2 == 1
        low = hidden.astype(BF)
        new = next_round()
        head_w[l] = head_rows(kinds)
        if l + 1 < layers:
            next_heads = lax.all_gather(later[l], "tensor", axis=1).reshape(4, g.nt * part, width)
        if windowed:
            far, seg_k, reach = near_rows(low), seg_near, halo
        else:
            far = far_inputs if l == 0 else far_rows(low)
            seg_k, reach = seg_far, 0
        q_w, k_w, v_w, o_w = head_w[l]
        query = [(dot_nt(low, w) + head_bias[l, 0, k]).astype(BF) for k, w in enumerate(q_w)]
        key = [dot_nt(far, w).astype(BF) for w in k_w]
        value = [(dot_nt(far, w) + head_bias[l, 1, k]).astype(BF) for k, w in enumerate(v_w)]
        context = [attend(*qkv, seg_q, seg_k, reach) for qkv in zip(query, key, value)]
        attended = hidden + out_bias[l]
        for a, w in zip(context, o_w):
            attended = attended + dot_nn(a, w)
        first_normal, first_inverse = norm_stats(attended)
        normed = first_normal * first_gain[l] + first_shift[l]
        normed_low = normed.astype(BF)
        normed, normed_low = end_round(new, (normed, normed_low))
        new = next_round()
        if l + 1 < layers:
            kinds = [next_heads[k] for k in range(4)]
        outer_now = new["unit_w"].get((l, "u"), unit_w.get((l, "u")))
        total, acts, slopes = feed_forward(normed_low, unit_w[l, "i"], outer_now, unit_bias[l])
        mixed = normed + outer_bias[l] + total
        second_normal, second_inverse = norm_stats(mixed)
        hidden = second_normal * second_gain[l] + second_shift[l]
        if l + 1 < layers:
            hidden, acts = end_round(new, (hidden, acts))
        else:
            end_round(new, ())
        swapped = [g.core(a) for a in [normed_low] + acts[g.nx :]]
        saved.append(
            (low, far, query, key, value, seg_k, reach, context, first_normal, first_inverse,
             normed_low, acts, slopes, second_normal, second_inverse, swapped)
        )
    result = hidden

    def unit_parts(mine, others, right):
        return [weight_grad(list(zip(both, right))) for both in zip(mine, others)]

    def sum_over_x(parts):
        for bit in g.bits("x")[::-1]:
            keep, give = parts[: len(parts) // 2], parts[len(parts) // 2 :]
            parts = [(a.astype(F32) + g.swap(b, "dp", bit).astype(F32)).astype(BF) for a, b in zip(keep, give)]
        return parts[0]

    def head_total(lefts, right):
        received = g.core(weight_grad([(lefts[1], right)])) if cores == 2 else None
        return weight_grad([(lefts[0], right)], received).reshape(g.nt, part, width)

    def head_steps(totals, bits):
        for bit in bits:
            keep, give = jnp.split(totals, 2)
            totals = (keep.astype(F32) + g.swap(give, "tensor", bit).astype(F32)).astype(BF)
        return totals

    def end_units(wide):
        wide = wide[None]
        for bit in g.bits("x"):
            wide = jnp.concatenate([wide, g.swap(wide, "dp", bit)])
        wide = jnp.stack([wide, g.core(wide)], 1)
        return g.turned(g.turned(wide, "x", 0), "c", 1)

    def end_heads(total):
        for bit in g.bits("x"):
            total = (total.astype(F32) + g.swap(total, "dp", bit).astype(F32)).astype(BF)
        if cores == 2:
            return g.turned(jnp.stack([total, g.core(total)]), "c", 0)
        return (total.astype(F32) + g.core(total).astype(F32))[None]

    unit_ends, head_ends, vectors = [[None, None] for _ in range(layers)], [None] * layers, [None] * layers
    grad_hidden = cotangent.astype(F32)
    shares = {}

    for l in reversed(range(layers)):
        (low, far, query, key, value, seg_k, reach, context, first_normal, first_inverse,
         normed_low, acts, slopes, second_normal, second_inverse, swapped) = saved[l]
        q_w, k_w, v_w, o_w = head_w[l]
        inner_w, outer_w = unit_w[l, "i"], unit_w[l, "u"]
        grad_mixed, d_second_gain, d_second_shift = norm_back(
            grad_hidden, second_normal, second_inverse, second_gain[l]
        )
        mixed_low = grad_mixed.astype(BF)
        d_outer_bias = jnp.sum(grad_mixed, axis=0)
        mixed_both = mixed_low, g.core(mixed_low)
        normed_both = normed_low, swapped[0]
        outer_parts = unit_parts(acts[: g.nx], swapped[1:], mixed_both)
        outer_parts, mixed_low, grad_mixed = together(outer_parts, mixed_low, grad_mixed)
        outer_sum = sum_over_x(outer_parts)
        total, d_inner_bias, grad_inner = feed_forward_back(mixed_low, inner_w, outer_w, slopes)
        inner_parts = unit_parts(grad_inner[: g.nx], [g.core(a) for a in grad_inner[g.nx :]], normed_both)
        grad_normed = grad_mixed + total
        grad_attended, d_first_gain, d_first_shift = norm_back(
            grad_normed, first_normal, first_inverse, first_gain[l]
        )
        outer_sum, inner_parts, grad_attended = together(outer_sum, inner_parts, grad_attended)
        inner_sum = sum_over_x(inner_parts)
        if l == 0:
            outer_sum = back_by_steps(outer_sum)
        d_out_bias = jnp.sum(grad_attended, axis=0)
        attended_low = grad_attended.astype(BF)
        grad_context = [dot_nt(attended_low, w).astype(BF) for w in o_w]
        out_total = head_total(context, attended_low)
        if l == 0:
            out_total = back_by_steps(out_total)
        backs = [
            attend_back(query[k], key[k], value[k], grad_context[k], seg_q, seg_k, reach) for k in range(cores)
        ]
        inner_sum, outer_sum, out_total, backs = together(inner_sum, outer_sum, out_total, backs)
        d_query, d_key, d_value = zip(*backs)
        if l == 0:
            v_total = back_by_steps(head_total(d_value, far))
        far_part = sum(
            dot_nn(a, w) for grad, weight in ((d_key, k_w), (d_value, v_w)) for a, w in zip(grad, weight)
        ).astype(BF)
        far_sum = near_sums(far_part) if reach else far_sums(far_part)
        near_sum = grad_attended
        for a, w in zip(d_query, q_w):
            near_sum = near_sum + dot_nn(a, w)
        grad_hidden = near_sum + far_sum
        q_total, k_total = head_total(d_query, low), head_total(d_key, far)
        if l == 0:
            shares[l, "iu"] = jnp.concatenate([back_by_steps(inner_sum), outer_sum])
            kinds = [back_by_steps(q_total), back_by_steps(k_total), v_total, out_total]
            head_ends[l] = jnp.concatenate([a.reshape(-1, width) for a in kinds])
        else:
            pack = jnp.stack([inner_sum.reshape(g.nt, block, width), outer_sum.reshape(g.nt, block, width)], 1)
            shares[l, "iu"] = lax.psum_scatter(
                pack.reshape(-1, width), "tensor", scatter_dimension=0, tiled=True
            )
            pack = jnp.concatenate([q_total, k_total, head_total(d_value, far), out_total], 1)
            head_ends[l] = lax.psum_scatter(
                pack.reshape(-1, width), "tensor", scatter_dimension=0, tiled=True
            )
        unit_order = d_inner_bias.reshape(2, g.nx, g.nt, block)
        unit_order = g.turned(g.turned(unit_order, "c", 0), "x", 1)
        if l == 0:
            unit_order = from_steps(unit_order, 2)
        head_grad = jnp.stack(
            [jnp.stack([jnp.sum(a, axis=0, dtype=F32) for a in grad]) for grad in (d_query, d_value)]
        ).reshape(2, cores, g.nt, part)
        if cores == 2:
            head_grad = g.turned(head_grad, "c", 1)
        if l == 0:
            head_grad = from_steps(head_grad, 2)
        vectors[l] = jnp.concatenate(
            [d_out_bias, d_first_gain, d_first_shift, d_outer_bias, d_second_gain, d_second_shift,
             jnp.transpose(unit_order, (2, 1, 0, 3)).reshape(-1),
             jnp.transpose(head_grad, (0, 2, 1, 3)).reshape(-1)]
        )

    vector = g.sum_all(jnp.stack(vectors))
    shared = [vector[:, k * width : (k + 1) * width] for k in range(6)]

    def own_part(start, count):
        return lax.dynamic_slice(vector, (0, start + g.tensor * count), (layers, count))

    d_inner_bias = own_part(6 * width, units)
    d_query_bias = own_part(6 * width + units * g.nt, heads)
    d_value_bias = own_part(6 * width + (units + heads) * g.nt, heads)

    ends = [
        (end_units(shares[l, "iu"]), end_heads(head_ends[l]))
        for l in range(layers)
    ]

    def shard(l, kind):
        wide, total = ends[l]
        if kind in "iu":
            k = "iu".index(kind)
            array = wide[:, :, k * block : (k + 1) * block].reshape(units, width)
        else:
            k = "qkvo".index(kind)
            array = total[:, k * part : (k + 1) * part].reshape(heads, width)
        return array

    kinds = [[shard(l, kind) for l in range(layers)] for kind in "qkviou"]
    d_query, d_key, d_value, d_inner, d_out, d_outer = gradients_out(kinds[:4], kinds[4:])
    return (
        result,
        grad_hidden,
        d_query,
        d_query_bias,
        d_key,
        d_value,
        d_value_bias,
        d_out,
        shared[0],
        shared[1],
        shared[2],
        d_inner,
        d_inner_bias,
        d_outer,
        shared[3],
        shared[4],
        shared[5],
    )


HINT = 1 << 16


def solution(mesh):
    rows = P(("dp", "tensor"), None)
    columns = P(None, None, "tensor")
    units = P(None, "tensor", None)
    vector = P(None, "tensor")
    in_specs = (
        rows, P("dp", None), columns, vector, columns, columns, vector, units, P(), P(), P(),
        columns, vector, units, P(), P(), P(), rows,
    )
    out_specs = (
        rows, rows, columns, vector, columns, columns, vector, units, P(), P(), P(),
        columns, vector, units, P(), P(), P(),
    )
    return jax.shard_map(
        partial(shards, Grid(mesh)), mesh=mesh, in_specs=in_specs, out_specs=out_specs, check_vma=False
    )
```

```python
from functools import partial

import jax
import jax.numpy as jnp
from jax import lax
from jax.experimental import pallas as pl
from jax.experimental.pallas import tpu as pltpu
from jax.sharding import PartitionSpec as P

HD = 64
WINDOW = 256
EPS = 1e-05
NEGATIVE = -1e30
BF = jnp.bfloat16
F32 = jnp.float32
LANES = 128


def dot_nn(left, right):
    return lax.dot_general(left, right, (((1,), (0,)), ((), ())), preferred_element_type=F32)


def dot_nt(left, right):
    return lax.dot_general(left, right, (((1,), (1,)), ((), ())), preferred_element_type=F32)


def dot_tn(left, right):
    return lax.dot_general(left, right, (((0,), (0,)), ((), ())), preferred_element_type=F32)


def allowed_keys(seg_q, seg_k, halo):
    allowed = seg_q == seg_k
    if halo:
        row = lax.broadcasted_iota(jnp.int32, allowed.shape, 0)
        col = lax.broadcasted_iota(jnp.int32, allowed.shape, 1)
        allowed = jnp.logical_and(allowed, jnp.abs(row + halo - col) <= WINDOW // 2)
    return allowed


def head_lanes(shape, head):
    lane = lax.broadcasted_iota(jnp.int32, shape, 1)
    return (lane // HD) == head


def probabilities(query, key, allowed):
    scores = jnp.where(allowed, dot_nt(query, key) * (HD ** -0.5), NEGATIVE)
    raised = jnp.exp(scores - jnp.max(scores, axis=-1, keepdims=True))
    return raised * (1.0 / jnp.sum(raised, axis=-1, keepdims=True))


def attend_kernel(halo, seg_q_ref, seg_k_ref, q_ref, k_ref, v_ref, c_ref):
    allowed = allowed_keys(seg_q_ref[...], seg_k_ref[...], halo)
    query, key, value = q_ref[...], k_ref[...], v_ref[...]
    total = None
    for head in range(LANES // HD):
        mine = head_lanes(query.shape, head)
        probs = probabilities(jnp.where(mine, query, jnp.zeros_like(query)), key, allowed)
        part = jnp.where(mine, dot_nn(probs.astype(BF), value), 0.0)
        total = part if total is None else total + part
    c_ref[...] = total.astype(BF)


def attend_back_kernel(halo, seg_q_ref, seg_k_ref, q_ref, k_ref, v_ref, g_ref, dq_ref, dk_ref, dv_ref):
    allowed = allowed_keys(seg_q_ref[...], seg_k_ref[...], halo)
    query, key, value, grad = q_ref[...], k_ref[...], v_ref[...], g_ref[...]
    dq = dk = dv = None
    for head in range(LANES // HD):
        mine = head_lanes(query.shape, head)
        own_q = jnp.where(mine, query, jnp.zeros_like(query))
        own_g = jnp.where(mine, grad, jnp.zeros_like(grad))
        probs = probabilities(own_q, key, allowed)
        grad_probs = dot_nt(own_g, value)
        delta = jnp.sum(probs * grad_probs, axis=-1, keepdims=True)
        grad_scores = (probs * (grad_probs - delta)).astype(BF)
        q_part = jnp.where(mine, dot_nn(grad_scores, key), 0.0)
        k_part = dot_tn(grad_scores, own_q)
        v_part = dot_tn(probs.astype(BF), own_g)
        dq = q_part if dq is None else dq + q_part
        dk = k_part if dk is None else dk + k_part
        dv = v_part if dv is None else dv + v_part
    dq_ref[...] = (dq * (HD ** -0.5)).astype(BF)
    dk_ref[...] = (dk * (HD ** -0.5)).astype(BF)
    dv_ref[...] = dv.astype(BF)


def attend(query, key, value, seg_q, seg_k, halo):
    rows, width = query.shape
    keys = key.shape[0]
    whole = lambda shape: pl.BlockSpec(shape, lambda p: (0, 0))
    near = pl.BlockSpec((rows, LANES), lambda p: (0, p))
    far = pl.BlockSpec((keys, LANES), lambda p: (0, p))
    return pl.pallas_call(
        partial(attend_kernel, halo),
        grid=(width // LANES,),
        in_specs=[whole((rows, 1)), whole((1, keys)), near, far, far],
        out_specs=near,
        out_shape=jax.ShapeDtypeStruct((rows, width), BF),
        compiler_params=pltpu.CompilerParams(vmem_limit_bytes=40 * 1024 * 1024),
        cost_estimate=hint(6.5 * keys / 1024),
        name="attend",
    )(seg_q, seg_k, query, key, value)


def attend_back(query, key, value, grad, seg_q, seg_k, halo):
    rows, width = query.shape
    keys = key.shape[0]
    whole = lambda shape: pl.BlockSpec(shape, lambda p: (0, 0))
    near = pl.BlockSpec((rows, LANES), lambda p: (0, p))
    far = pl.BlockSpec((keys, LANES), lambda p: (0, p))
    return pl.pallas_call(
        partial(attend_back_kernel, halo),
        grid=(width // LANES,),
        in_specs=[whole((rows, 1)), whole((1, keys)), near, far, far, near],
        out_specs=[near, far, far],
        out_shape=[
            jax.ShapeDtypeStruct((rows, width), BF),
            jax.ShapeDtypeStruct((keys, width), BF),
            jax.ShapeDtypeStruct((keys, width), BF),
        ],
        compiler_params=pltpu.CompilerParams(vmem_limit_bytes=48 * 1024 * 1024),
        cost_estimate=hint(10.0 * keys / 1024),
        name="attend_back",
    )(seg_q, seg_k, query, key, value, grad)


def norm_stats(values):
    center = values - jnp.mean(values, axis=-1, keepdims=True)
    inverse = lax.rsqrt(jnp.mean(center * center, axis=-1, keepdims=True) + EPS)
    return center * inverse, inverse


def norm_back(grad, normal, inverse, gain):
    scaled = grad * gain
    back = inverse * (
        scaled
        - jnp.mean(scaled, axis=-1, keepdims=True)
        - normal * jnp.mean(scaled * normal, axis=-1, keepdims=True)
    )
    return back, jnp.sum(grad * normal, axis=0), jnp.sum(grad, axis=0)


def gelu_and_slope(inner):
    half = 0.5 * (1.0 + lax.erf(inner * (0.5 ** 0.5)))
    bell = jnp.exp(-0.5 * inner * inner) * ((2.0 * jnp.pi) ** -0.5)
    return (inner * half).astype(BF), (half + inner * bell).astype(BF)


def hint(us):
    return pl.CostEstimate(flops=0, bytes_accessed=int(us * 1.3e6), transcendentals=0)


def streamed(kernel_step, near, first, second, extra, outs, name):
    count, (rows_of, width) = len(first), first[0].shape
    tile = min(512, rows_of)
    steps = [(k, t * tile) for k in range(count) for t in range(rows_of // tile)]
    near_count, extra_count = len(near), len(extra)

    def kernel(*refs):
        near_refs, refs = refs[:near_count], refs[near_count:]
        extra_refs, refs = refs[:extra_count], refs[extra_count:]
        one_refs, two_refs, refs = refs[:count], refs[count : 2 * count], refs[2 * count :]
        *out_refs, one_held, two_held, sems = refs

        def copies(s):
            k, at = steps[s]
            slot = s % 2
            return [
                pltpu.make_async_copy(one_refs[k].at[pl.ds(at, tile)], one_held.at[slot], sems.at[0, slot]),
                pltpu.make_async_copy(two_refs[k].at[pl.ds(at, tile)], two_held.at[slot], sems.at[1, slot]),
            ]

        for copy in copies(0):
            copy.start()
        for s, (k, at) in enumerate(steps):
            if s + 1 < len(steps):
                for copy in copies(s + 1):
                    copy.start()
            for copy in copies(s):
                copy.wait()
            kernel_step(s, k, at, tile, near_refs, extra_refs, one_held.at[s % 2], two_held.at[s % 2], out_refs)

    whole = pl.BlockSpec(memory_space=pltpu.VMEM)
    anywhere = pl.BlockSpec(memory_space=pl.ANY)
    dtype = first[0].dtype
    return pl.pallas_call(
        kernel,
        in_specs=[whole] * (near_count + extra_count) + [anywhere] * (2 * count),
        out_specs=[whole] * len(outs),
        out_shape=outs,
        scratch_shapes=[
            pltpu.VMEM((2, tile, width), dtype),
            pltpu.VMEM((2, tile, width), dtype),
            pltpu.SemaphoreType.DMA((2, 2)),
        ],
        compiler_params=pltpu.CompilerParams(vmem_limit_bytes=40 * 1024 * 1024),
        cost_estimate=hint(10.0),
        name=name,
    )(*near, *extra, *first, *second)


def feed_forward(rows_low, inner, outer, bias):
    count, (each, width), rows = len(inner), inner[0].shape, rows_low.shape[0]

    def step(s, k, at, tile, near, extra, inner_tile, outer_tile, outs):
        act, slope = gelu_and_slope(
            dot_nt(near[0][...], inner_tile[...]) + extra[0][pl.ds(k, 1), pl.ds(at, tile)]
        )
        outs[1 + k][:, pl.ds(at, tile)] = act
        outs[1 + count + k][:, pl.ds(at, tile)] = slope
        part = dot_nn(act, outer_tile[...])
        outs[0][...] = part if s == 0 else outs[0][...] + part

    shapes = [jax.ShapeDtypeStruct((rows, width), F32)] + [jax.ShapeDtypeStruct((rows, each), BF)] * (2 * count)
    total, *rest = streamed(step, [rows_low], inner, outer, [bias], shapes, "feed_forward")
    return total, rest[:count], rest[count:]


def feed_forward_back(grad_low, inner, outer, slopes):
    count, (each, width), rows = len(inner), inner[0].shape, grad_low.shape[0]

    def step(s, k, at, tile, near, extra, outer_tile, inner_tile, outs):
        grad = (dot_nt(near[0][...], outer_tile[...]) * extra[k][:, pl.ds(at, tile)].astype(F32)).astype(BF)
        outs[2 + k][:, pl.ds(at, tile)] = grad
        outs[1][pl.ds(k, 1), pl.ds(at, tile)] = jnp.sum(grad.astype(F32), axis=0, keepdims=True)
        part = dot_nn(grad, inner_tile[...])
        outs[0][...] = part if s == 0 else outs[0][...] + part

    shapes = [jax.ShapeDtypeStruct((rows, width), F32), jax.ShapeDtypeStruct((count, each), F32)]
    shapes += [jax.ShapeDtypeStruct((rows, each), BF)] * count
    total, sums, *grads = streamed(step, [grad_low], outer, inner, list(slopes), shapes, "feed_forward_back")
    return total, sums, grads


def weight_grad(pairs, add=None):
    columns, width = pairs[0][0].shape[1], pairs[0][1].shape[1]
    tile = min(256, columns)

    def kernel(*refs):
        total = None
        for k in range(len(pairs)):
            part = dot_tn(refs[2 * k][...], refs[2 * k + 1][...])
            total = part if total is None else total + part
        if add is not None:
            total = total + refs[2 * len(pairs)][...].astype(F32)
        refs[-1][...] = total.astype(BF)

    block = pl.BlockSpec((tile, width), lambda t: (t, 0))
    specs, operands = [], []
    for left, right in pairs:
        specs += [
            pl.BlockSpec((left.shape[0], tile), lambda t: (0, t)),
            pl.BlockSpec(right.shape, lambda t: (0, 0)),
        ]
        operands += [left, right]
    if add is not None:
        specs.append(block)
        operands.append(add)
    return pl.pallas_call(
        kernel,
        grid=(columns // tile,),
        in_specs=specs,
        out_specs=block,
        out_shape=jax.ShapeDtypeStruct((columns, width), BF),
        compiler_params=pltpu.CompilerParams(vmem_limit_bytes=32 * 1024 * 1024),
        cost_estimate=hint(2.0 * sum(a.shape[0] for a, _ in pairs) * columns / (512 * 1024)),
        name="weight_grad",
    )(*operands)


def gradients_out(turned, plain):
    layers, width = len(turned[0]), turned[0][0].shape[1]
    steps = 4

    def kernel(*refs):
        outs = refs[layers * (len(turned) + len(plain)) :]
        for k, out in enumerate(outs):
            for l in range(layers):
                value = refs[k * layers + l][...].astype(F32)
                out[l] = value.T if k < len(turned) else value

    specs, shapes, out_specs = [], [], []
    for arrays in turned:
        rows = arrays[0].shape[0]
        specs += [pl.BlockSpec((rows, width // steps), lambda t: (0, t))] * layers
        out_specs.append(pl.BlockSpec((layers, width // steps, rows), lambda t: (0, t, 0)))
        shapes.append(jax.ShapeDtypeStruct((layers, width, rows), F32))
    for arrays in plain:
        rows = arrays[0].shape[0]
        specs += [pl.BlockSpec((rows // steps, width), lambda t: (t, 0))] * layers
        out_specs.append(pl.BlockSpec((layers, rows // steps, width), lambda t: (0, t, 0)))
        shapes.append(jax.ShapeDtypeStruct((layers, rows, width), F32))
    return pl.pallas_call(
        kernel,
        grid=(steps,),
        in_specs=specs,
        out_specs=out_specs,
        out_shape=shapes,
        compiler_params=pltpu.CompilerParams(vmem_limit_bytes=40 * 1024 * 1024),
        cost_estimate=hint(5.0),
        name="gradients_out",
    )(*[a for arrays in turned + plain for a in arrays])


class Grid:
    def __init__(self, mesh):
        self.nd, self.nt = mesh.shape["dp"], mesh.shape["tensor"]
        self.nx = self.nd // 2

    def place(self):
        self.dp, self.tensor = lax.axis_index("dp"), lax.axis_index("tensor")
        self.x, self.c = self.dp // 2, self.dp % 2

    def swap(self, array, axis, bit):
        count = self.nd if axis == "dp" else self.nt
        return lax.ppermute(array, axis, [(i, i ^ bit) for i in range(count)])

    def core(self, array):
        return self.swap(array, "dp", 1)

    def bits(self, name):
        low, high = {"x": (2, self.nd), "t": (1, self.nt)}[name]
        found = []
        while low < high:
            found.append(low)
            low *= 2
        return found

    def shift(self, array, by, group):
        pairs = [(i, i + by) for i in range(self.nt) if 0 <= i + by < self.nt and i // group == (i + by) // group]
        return lax.ppermute(array, "tensor", pairs)

    def turned(self, array, name, axis):
        count, at = {"x": (self.nx, self.x), "c": (2, self.c), "t": (self.nt, self.tensor)}[name]
        if count == 2:
            return jnp.where(at == 0, array, lax.rev(array, (axis,)))
        return jnp.take(array, at ^ jnp.arange(count), axis=axis)


def together(*values):
    return lax.optimization_barrier(values)


def shards(
    grid,
    inputs,
    segments,
    query_weight,
    query_bias,
    key_weight,
    value_weight,
    value_bias,
    out_weight,
    out_bias,
    first_gain,
    first_shift,
    inner_weight,
    inner_bias,
    outer_weight,
    outer_bias,
    second_gain,
    second_shift,
    cotangent,
):
    g = grid
    g.place()
    layers = query_weight.shape[0]
    rows, width = inputs.shape
    heads = query_weight.shape[2]
    cores = 2 if heads // 2 % HD == 0 else 1
    part = heads // cores
    units = inner_weight.shape[2]
    block = units // g.nd
    length = segments.shape[1]
    group = length // rows
    halo = WINDOW // 2
    high_to_low = g.bits("t")[::-1]

    own = segments[g.tensor // group] if segments.shape[0] > 1 else segments[0]
    spot = g.tensor % group
    seg_q = lax.dynamic_slice(own, (spot * rows,), (rows,))[:, None]
    padded = jnp.pad(own, (halo, halo), constant_values=-1)
    seg_near = lax.dynamic_slice(padded, (spot * rows,), (rows + 2 * halo,))[None]
    seg_far = jnp.take(own.reshape(group, rows), spot ^ jnp.arange(group), axis=0).reshape(1, length)

    def far_rows(array, other=None):
        bit = 1
        while bit < group:
            if other is None:
                other = g.swap(array, "tensor", bit)
            array, other = jnp.concatenate([array, other]), None
            bit *= 2
        return array

    def far_sums(array):
        bit = group // 2
        while bit:
            keep, give = jnp.split(array, 2)
            array = keep.astype(F32) + g.swap(give.astype(BF), "tensor", bit).astype(F32)
            bit //= 2
        return array

    def near_rows(array):
        return jnp.concatenate(
            [g.shift(array[rows - halo :], 1, group), array, g.shift(array[:halo], -1, group)]
        )

    def near_sums(array):
        after_rows = g.shift(array[:halo], -1, group).astype(F32)
        before_rows = g.shift(array[rows + halo :], 1, group).astype(F32)
        edge = jnp.zeros((rows - halo, width), F32)
        return (
            array[halo : rows + halo].astype(F32)
            + jnp.concatenate([edge, after_rows])
            + jnp.concatenate([before_rows, edge])
        )

    step_order = [0]
    for bit in high_to_low:
        step_order = step_order + [m | bit for m in step_order]
    blocks = 2 * g.nx

    def by_steps(array):
        for bit in high_to_low:
            array = jnp.concatenate([array, g.swap(array, "tensor", bit)])
        return array

    def from_steps(array, axis):
        place = jnp.array([step_order.index(m) for m in range(g.nt)])
        return jnp.take(array, place[g.tensor ^ jnp.arange(g.nt)], axis=axis)

    def unit_piece(shard):
        return lax.dynamic_index_in_dim(shard.reshape(g.nd, block, width), g.dp, 0, keepdims=False)

    def over_x(array):
        pieces = [array]
        for bit in g.bits("x"):
            pieces = pieces + [g.swap(a, "dp", bit) for a in pieces]
        return pieces

    def over_core(pieces):
        return pieces + [g.core(a) for a in pieces]

    def head_piece(l):
        pack = jnp.stack([query_weight[l].T, key_weight[l].T, value_weight[l].T, out_weight[l]])
        if cores == 2:
            pack = lax.dynamic_index_in_dim(pack.reshape(4, 2, part, width), g.c, 1, keepdims=False)
        return pack.reshape(1, 4 * part, width)

    def head_first(pack):
        for bit in high_to_low[:-1]:
            pack = jnp.concatenate([pack, g.swap(pack, "tensor", bit)])
        return pack

    def head_last(pack):
        both = [pack, g.swap(pack, "tensor", high_to_low[-1])]
        return [
            jnp.concatenate([a[:, k * part : (k + 1) * part].reshape(-1, width) for a in both]) for k in range(4)
        ]

    def head_rows(kinds):
        return [[a] if cores == 1 else [a, g.core(a)] for a in kinds]

    def bias_rows():
        pack = by_steps(jnp.concatenate([inner_bias, query_bias, value_bias], axis=1)[None])
        unit = pack[..., :units].reshape(g.nt, layers, g.nx, 2, block)
        unit = g.turned(g.turned(unit, "x", 2), "c", 3)
        head = pack[..., units:].reshape(g.nt, layers, 2, cores, part)
        if cores == 2:
            head = g.turned(head, "c", 3)
        unit = jnp.concatenate([unit[:, :1], from_steps(unit[:, 1:], 0)], 1)
        head = jnp.concatenate([head[:, :1], from_steps(head[:, 1:], 0)], 1)
        unit = jnp.transpose(unit, (1, 3, 2, 0, 4)).reshape(layers, blocks, -1)
        return unit, jnp.transpose(head, (1, 2, 3, 0, 4)).reshape(layers, 2, cores, -1)

    moves = [(l, kind) for l in range(layers) for kind in "iu"]
    shard_of = {(l, kind): {"i": inner_weight[l].T, "u": outer_weight[l]}[kind] for l, kind in moves}
    piece_of, gathered, spread, unit_w, head_w = {}, {}, {}, {}, {}
    piece_of[moves[0]] = unit_piece(shard_of[moves[0]])
    stage = 0

    def next_round():
        nonlocal stage
        new = {"piece_of": {}, "gathered": {}, "spread": {}, "unit_w": {}}
        for back, name in enumerate(new):
            if 0 <= stage + 1 - back < len(moves):
                key = moves[stage + 1 - back]
                if back > 1 or key[0] == 0:
                    new[name][key] = (
                        unit_piece(shard_of[key]) if back == 0
                        else by_steps(piece_of[key]) if back == 1
                        else over_x(gathered[key]) if back == 2
                        else over_core(spread[key])
                    )
        stage += 1
        return new

    def end_round(new, carry):
        new, carry = together(new, carry)
        for name, kept in (("piece_of", piece_of), ("gathered", gathered), ("spread", spread), ("unit_w", unit_w)):
            kept.update(new[name])
        return carry

    saved = []
    hidden = inputs.astype(F32)
    new = next_round()
    unit_bias, head_bias = bias_rows()
    far = g.swap(inputs, "tensor", 1) if group > 1 else inputs
    first_part = head_first(head_piece(0))
    later = [
        (jnp.stack([unit_piece(shard_of[l, "i"]), unit_piece(shard_of[l, "u"])]), head_piece(l).reshape(4, part, width))
        for l in range(1, layers)
    ]
    unit_bias, head_bias, far, first_part, later = end_round(new, (unit_bias, head_bias, far, first_part, later))
    for l in range(1, layers):
        both = lax.all_gather(later[l - 1][0], "tensor", axis=0)
        for k, kind in enumerate("iu"):
            gathered[l, kind] = both[:, k].reshape(-1, width)
    new = next_round()
    far_inputs = far_rows(inputs, far)
    kinds = head_last(first_part)
    hidden, far_inputs, kinds, later = end_round(new, (hidden, far_inputs, kinds, later))
    for l in range(layers):
        windowed = l % 2 == 1
        low = hidden.astype(BF)
        new = next_round()
        head_w[l] = head_rows(kinds)
        if l + 1 < layers:
            next_heads = lax.all_gather(later[l][1], "tensor", axis=1).reshape(4, g.nt * part, width)
        if windowed:
            far, seg_k, reach = near_rows(low), seg_near, halo
        else:
            far = far_inputs if l == 0 else far_rows(low)
            seg_k, reach = seg_far, 0
        q_w, k_w, v_w, o_w = head_w[l]
        query = [(dot_nt(low, w) + head_bias[l, 0, k]).astype(BF) for k, w in enumerate(q_w)]
        key = [dot_nt(far, w).astype(BF) for w in k_w]
        value = [(dot_nt(far, w) + head_bias[l, 1, k]).astype(BF) for k, w in enumerate(v_w)]
        context = [attend(*qkv, seg_q, seg_k, reach) for qkv in zip(query, key, value)]
        attended = hidden + out_bias[l]
        for a, w in zip(context, o_w):
            attended = attended + dot_nn(a, w)
        first_normal, first_inverse = norm_stats(attended)
        normed = first_normal * first_gain[l] + first_shift[l]
        normed_low = normed.astype(BF)
        normed, normed_low = end_round(new, (normed, normed_low))
        new = next_round()
        if l + 1 < layers:
            kinds = [next_heads[k] for k in range(4)]
        outer_now = new["unit_w"].get((l, "u"), unit_w.get((l, "u")))
        total, acts, slopes = feed_forward(normed_low, unit_w[l, "i"], outer_now, unit_bias[l])
        mixed = normed + outer_bias[l] + total
        second_normal, second_inverse = norm_stats(mixed)
        hidden = second_normal * second_gain[l] + second_shift[l]
        if l + 1 < layers:
            hidden, acts = end_round(new, (hidden, acts))
        else:
            end_round(new, ())
        swapped = [g.core(a) for a in [normed_low] + acts[g.nx :]]
        saved.append(
            (low, far, query, key, value, seg_k, reach, context, first_normal, first_inverse,
             normed_low, acts, slopes, second_normal, second_inverse, swapped)
        )
    result = hidden

    def unit_parts(mine, others, right):
        return [weight_grad(list(zip(both, right))) for both in zip(mine, others)]

    def sum_over_x(parts):
        for bit in g.bits("x")[::-1]:
            keep, give = parts[: len(parts) // 2], parts[len(parts) // 2 :]
            parts = [(a.astype(F32) + g.swap(b, "dp", bit).astype(F32)).astype(BF) for a, b in zip(keep, give)]
        return parts[0]

    def head_total(lefts, right):
        received = g.core(weight_grad([(lefts[1], right)])) if cores == 2 else None
        return weight_grad([(lefts[0], right)], received).reshape(g.nt, part, width)

    def one_step(total, bit):
        keep, give = jnp.split(total, 2)
        return (keep.astype(F32) + g.swap(give, "tensor", bit).astype(F32)).astype(BF)

    def end_over_x(wide, total):
        wide = wide[None]
        for bit in g.bits("x"):
            wide = jnp.concatenate([wide, g.swap(wide, "dp", bit)])
            total = (total.astype(F32) + g.swap(total, "dp", bit).astype(F32)).astype(BF)
        return wide, total

    def end_over_core(wide, total):
        wide = jnp.stack([wide, g.core(wide)], 1)
        wide = g.turned(g.turned(wide, "x", 0), "c", 1)
        if cores == 2:
            return wide, g.turned(jnp.stack([total, g.core(total)]), "c", 0)
        return wide, (total.astype(F32) + g.core(total).astype(F32))[None]

    ends, vectors, later_units = [None] * layers, [None] * layers, [None] * layers
    grad_hidden = cotangent.astype(F32)
    units_before = None
    first_bits = high_to_low[::-1]
    for l in reversed(range(layers)):
        (low, far, query, key, value, seg_k, reach, context, first_normal, first_inverse,
         normed_low, acts, slopes, second_normal, second_inverse, swapped) = saved[l]
        q_w, k_w, v_w, o_w = head_w[l]
        inner_w, outer_w = unit_w[l, "i"], unit_w[l, "u"]
        grad_mixed, d_second_gain, d_second_shift = norm_back(
            grad_hidden, second_normal, second_inverse, second_gain[l]
        )
        mixed_low = grad_mixed.astype(BF)
        d_outer_bias = jnp.sum(grad_mixed, axis=0)
        mixed_both = mixed_low, g.core(mixed_low)
        normed_both = normed_low, swapped[0]
        outer_parts = unit_parts(acts[: g.nx], swapped[1:], mixed_both)
        outer_parts, mixed_low, grad_mixed, units_before = together(
            outer_parts, mixed_low, grad_mixed, units_before
        )
        if units_before is not None:
            pack = jnp.stack(units_before, 1)
            later_units[l + 1] = lax.psum_scatter(
                pack.reshape(-1, width), "tensor", scatter_dimension=0, tiled=True
            )
        outer_sum = sum_over_x(outer_parts).reshape(g.nt, block, width)
        total, d_inner_bias, grad_inner = feed_forward_back(mixed_low, inner_w, outer_w, slopes)
        inner_parts = unit_parts(grad_inner[: g.nx], [g.core(a) for a in grad_inner[g.nx :]], normed_both)
        grad_normed = grad_mixed + total
        grad_attended, d_first_gain, d_first_shift = norm_back(
            grad_normed, first_normal, first_inverse, first_gain[l]
        )
        inner_parts, grad_attended = together(inner_parts, grad_attended)
        inner_sum = sum_over_x(inner_parts).reshape(g.nt, block, width)
        d_out_bias = jnp.sum(grad_attended, axis=0)
        attended_low = grad_attended.astype(BF)
        grad_context = [dot_nt(attended_low, w).astype(BF) for w in o_w]
        out_total = head_total(context, attended_low)
        backs = []
        for k in range(cores):
            backs.append(attend_back(query[k], key[k], value[k], grad_context[k], seg_q, seg_k, reach))
            if k == 0:
                backs, outer_sum, grad_context, out_total = together(backs, outer_sum, grad_context, out_total)
            elif l == 0:
                outer_sum, out_total = one_step(outer_sum, first_bits[0]), one_step(out_total, first_bits[0])
        backs, outer_sum, out_total = together(backs, outer_sum, out_total)
        d_query, d_key, d_value = zip(*backs)
        far_part = sum(
            dot_nn(a, w) for grad, weight in ((d_key, k_w), (d_value, v_w)) for a, w in zip(grad, weight)
        ).astype(BF)
        near_sum = grad_attended
        for a, w in zip(d_query, q_w):
            near_sum = near_sum + dot_nn(a, w)
        v_total = head_total(d_value, far)
        totals = [head_total(d_query, low), head_total(d_key, far), v_total]
        unit_order = d_inner_bias.reshape(2, g.nx, g.nt, block)
        unit_order = g.turned(g.turned(unit_order, "c", 0), "x", 1)
        if l == 0:
            unit_order = from_steps(unit_order, 2)
        head_grad = jnp.stack(
            [jnp.stack([jnp.sum(a, axis=0, dtype=F32) for a in grad]) for grad in (d_query, d_value)]
        ).reshape(2, cores, g.nt, part)
        if cores == 2:
            head_grad = g.turned(head_grad, "c", 1)
        if l == 0:
            head_grad = from_steps(head_grad, 2)
        vectors[l] = jnp.concatenate(
            [d_out_bias, d_first_gain, d_first_shift, d_outer_bias, d_second_gain, d_second_shift,
             jnp.transpose(unit_order, (2, 1, 0, 3)).reshape(-1),
             jnp.transpose(head_grad, (0, 2, 1, 3)).reshape(-1)]
        )
        if l:
            far_sum = near_sums(far_part) if reach else far_sums(far_part)
            grad_hidden = near_sum + far_sum
            pack = jnp.concatenate([*totals, out_total], 1)
            ends[l] = lax.psum_scatter(pack.reshape(-1, width), "tensor", scatter_dimension=0, tiled=True)
            units_before = inner_sum, outer_sum
    steps_done = cores - 1
    vector = jnp.stack(vectors)
    hops = [(axis, 1 << k) for axis, count in (("dp", g.nd), ("tensor", g.nt)) for k in range(count.bit_length() - 1)]
    far_bits = [1 << k for k in range(group.bit_length() - 1)][::-1]

    def next_hop(vector):
        return vector + g.swap(vector, *hops.pop(0)) if hops else vector

    for bit in first_bits[steps_done : steps_done + 1]:
        outer_sum, out_total = one_step(outer_sum, bit), one_step(out_total, bit)
    inner_sum, totals[2] = one_step(inner_sum, first_bits[0]), one_step(totals[2], first_bits[0])
    totals, outer_sum, out_total, inner_sum, vector, far_part = together(
        totals, outer_sum, out_total, inner_sum, vector, far_part
    )
    for number, bit in enumerate(first_bits):
        totals[:2] = [one_step(a, bit) for a in totals[:2]]
        if number + 1 < len(first_bits):
            inner_sum = one_step(inner_sum, first_bits[number + 1])
            totals[2] = one_step(totals[2], first_bits[number + 1])
        if number + steps_done + 1 < len(first_bits):
            more = first_bits[number + steps_done + 1]
            outer_sum, out_total = one_step(outer_sum, more), one_step(out_total, more)
        vector = next_hop(vector)
        if far_bits:
            keep, give = jnp.split(far_part, 2)
            far_part = keep.astype(F32) + g.swap(give.astype(BF), "tensor", far_bits.pop(0)).astype(F32)
        if number == 1:
            for l in range(1, layers):
                ends[l] = end_over_x(later_units[l], ends[l])
        if number == 2:
            for l in range(1, layers):
                ends[l] = end_over_core(*ends[l])
        totals, outer_sum, out_total, inner_sum, vector, far_part, ends = together(
            totals, outer_sum, out_total, inner_sum, vector, far_part, ends
        )
    while far_bits:
        keep, give = jnp.split(far_part, 2)
        far_part = keep.astype(F32) + g.swap(give.astype(BF), "tensor", far_bits.pop(0)).astype(F32)
    grad_hidden = near_sum + far_part
    wide = jnp.concatenate([a.reshape(-1, width) for a in (inner_sum, outer_sum)])
    total = jnp.concatenate([a.reshape(-1, width) for a in (*totals, out_total)])
    vector = next_hop(vector)
    wide, total, vector = together(*end_over_x(wide, total), vector)
    ends[0] = end_over_core(wide, total)
    while hops:
        vector = next_hop(vector)

    shared = [vector[:, k * width : (k + 1) * width] for k in range(6)]

    def own_part(start, count):
        return lax.dynamic_slice(vector, (0, start + g.tensor * count), (layers, count))

    d_inner_bias = own_part(6 * width, units)
    d_query_bias = own_part(6 * width + units * g.nt, heads)
    d_value_bias = own_part(6 * width + (units + heads) * g.nt, heads)

    def shard(l, kind):
        wide, total = ends[l]
        if kind in "iu":
            k = "iu".index(kind)
            array = wide[:, :, k * block : (k + 1) * block].reshape(units, width)
        else:
            k = "qkvo".index(kind)
            array = total[:, k * part : (k + 1) * part].reshape(heads, width)
        return array

    kinds = [[shard(l, kind) for l in range(layers)] for kind in "qkviou"]
    d_query, d_key, d_value, d_inner, d_out, d_outer = gradients_out(kinds[:4], kinds[4:])
    return (
        result,
        grad_hidden,
        d_query,
        d_query_bias,
        d_key,
        d_value,
        d_value_bias,
        d_out,
        shared[0],
        shared[1],
        shared[2],
        d_inner,
        d_inner_bias,
        d_outer,
        shared[3],
        shared[4],
        shared[5],
    )


def solution(mesh):
    rows = P(("dp", "tensor"), None)
    columns = P(None, None, "tensor")
    units = P(None, "tensor", None)
    vector = P(None, "tensor")
    in_specs = (
        rows, P("dp", None), columns, vector, columns, columns, vector, units, P(), P(), P(),
        columns, vector, units, P(), P(), P(), rows,
    )
    out_specs = (
        rows, rows, columns, vector, columns, columns, vector, units, P(), P(), P(),
        columns, vector, units, P(), P(), P(),
    )
    return jax.shard_map(
        partial(shards, Grid(mesh)), mesh=mesh, in_specs=in_specs, out_specs=out_specs, check_vma=False
    )
```

```python
from functools import partial

import jax
import jax.numpy as jnp
from jax import lax
from jax.experimental import pallas as pl
from jax.experimental.pallas import tpu as pltpu
from jax.sharding import PartitionSpec as P

HD = 64
WINDOW = 256
EPS = 1e-05
NEGATIVE = -1e30
BF = jnp.bfloat16
F32 = jnp.float32
LANES = 128


def dot_nn(left, right):
    return lax.dot_general(left, right, (((1,), (0,)), ((), ())), preferred_element_type=F32)


def dot_nt(left, right):
    return lax.dot_general(left, right, (((1,), (1,)), ((), ())), preferred_element_type=F32)


def dot_tn(left, right):
    return lax.dot_general(left, right, (((0,), (0,)), ((), ())), preferred_element_type=F32)


def allowed_keys(seg_q, seg_k, halo):
    allowed = seg_q == seg_k
    if halo:
        row = lax.broadcasted_iota(jnp.int32, allowed.shape, 0)
        col = lax.broadcasted_iota(jnp.int32, allowed.shape, 1)
        allowed = jnp.logical_and(allowed, jnp.abs(row + halo - col) <= WINDOW // 2)
    return allowed


def head_lanes(shape, head):
    lane = lax.broadcasted_iota(jnp.int32, shape, 1)
    return (lane // HD) == head


def probabilities(query, key, allowed):
    scores = jnp.where(allowed, dot_nt(query, key) * (HD ** -0.5), NEGATIVE)
    raised = jnp.exp(scores - jnp.max(scores, axis=-1, keepdims=True))
    return raised * (1.0 / jnp.sum(raised, axis=-1, keepdims=True))


def attend_kernel(halo, seg_q_ref, seg_k_ref, q_ref, k_ref, v_ref, c_ref):
    allowed = allowed_keys(seg_q_ref[...], seg_k_ref[...], halo)
    query, key, value = q_ref[...], k_ref[...], v_ref[...]
    total = None
    for head in range(LANES // HD):
        mine = head_lanes(query.shape, head)
        probs = probabilities(jnp.where(mine, query, jnp.zeros_like(query)), key, allowed)
        part = jnp.where(mine, dot_nn(probs.astype(BF), value), 0.0)
        total = part if total is None else total + part
    c_ref[...] = total.astype(BF)


def attend_back_kernel(halo, seg_q_ref, seg_k_ref, q_ref, k_ref, v_ref, g_ref, dq_ref, dk_ref, dv_ref):
    allowed = allowed_keys(seg_q_ref[...], seg_k_ref[...], halo)
    query, key, value, grad = q_ref[...], k_ref[...], v_ref[...], g_ref[...]
    dq = dk = dv = None
    for head in range(LANES // HD):
        mine = head_lanes(query.shape, head)
        own_q = jnp.where(mine, query, jnp.zeros_like(query))
        own_g = jnp.where(mine, grad, jnp.zeros_like(grad))
        probs = probabilities(own_q, key, allowed)
        grad_probs = dot_nt(own_g, value)
        delta = jnp.sum(probs * grad_probs, axis=-1, keepdims=True)
        grad_scores = (probs * (grad_probs - delta)).astype(BF)
        q_part = jnp.where(mine, dot_nn(grad_scores, key), 0.0)
        k_part = dot_tn(grad_scores, own_q)
        v_part = dot_tn(probs.astype(BF), own_g)
        dq = q_part if dq is None else dq + q_part
        dk = k_part if dk is None else dk + k_part
        dv = v_part if dv is None else dv + v_part
    dq_ref[...] = (dq * (HD ** -0.5)).astype(BF)
    dk_ref[...] = (dk * (HD ** -0.5)).astype(BF)
    dv_ref[...] = dv.astype(BF)


def attend(query, key, value, seg_q, seg_k, halo):
    rows, width = query.shape
    keys = key.shape[0]
    whole = lambda shape: pl.BlockSpec(shape, lambda p: (0, 0))
    near = pl.BlockSpec((rows, LANES), lambda p: (0, p))
    far = pl.BlockSpec((keys, LANES), lambda p: (0, p))
    return pl.pallas_call(
        partial(attend_kernel, halo),
        grid=(width // LANES,),
        in_specs=[whole((rows, 1)), whole((1, keys)), near, far, far],
        out_specs=near,
        out_shape=jax.ShapeDtypeStruct((rows, width), BF),
        compiler_params=pltpu.CompilerParams(vmem_limit_bytes=40 * 1024 * 1024),
        cost_estimate=hint(6.5 * keys / 1024),
        name="attend",
    )(seg_q, seg_k, query, key, value)


def attend_back(query, key, value, grad, seg_q, seg_k, halo):
    rows, width = query.shape
    keys = key.shape[0]
    whole = lambda shape: pl.BlockSpec(shape, lambda p: (0, 0))
    near = pl.BlockSpec((rows, LANES), lambda p: (0, p))
    far = pl.BlockSpec((keys, LANES), lambda p: (0, p))
    return pl.pallas_call(
        partial(attend_back_kernel, halo),
        grid=(width // LANES,),
        in_specs=[whole((rows, 1)), whole((1, keys)), near, far, far, near],
        out_specs=[near, far, far],
        out_shape=[
            jax.ShapeDtypeStruct((rows, width), BF),
            jax.ShapeDtypeStruct((keys, width), BF),
            jax.ShapeDtypeStruct((keys, width), BF),
        ],
        compiler_params=pltpu.CompilerParams(vmem_limit_bytes=48 * 1024 * 1024),
        cost_estimate=hint(10.0 * keys / 1024),
        name="attend_back",
    )(seg_q, seg_k, query, key, value, grad)


def norm_stats(values):
    center = values - jnp.mean(values, axis=-1, keepdims=True)
    inverse = lax.rsqrt(jnp.mean(center * center, axis=-1, keepdims=True) + EPS)
    return center * inverse, inverse


def norm_back(grad, normal, inverse, gain):
    scaled = grad * gain
    back = inverse * (
        scaled
        - jnp.mean(scaled, axis=-1, keepdims=True)
        - normal * jnp.mean(scaled * normal, axis=-1, keepdims=True)
    )
    return back, jnp.sum(grad * normal, axis=0), jnp.sum(grad, axis=0)


def gelu_and_slope(inner):
    half = 0.5 * (1.0 + lax.erf(inner * (0.5 ** 0.5)))
    bell = jnp.exp(-0.5 * inner * inner) * ((2.0 * jnp.pi) ** -0.5)
    return (inner * half).astype(BF), (half + inner * bell).astype(BF)


def hint(us):
    return pl.CostEstimate(flops=0, bytes_accessed=int(us * 1.3e6), transcendentals=0)


def streamed(kernel_step, near, first, second, extra, outs, name):
    count, (rows_of, width) = len(first), first[0].shape
    tile = min(512, rows_of)
    steps = [(k, t * tile) for k in range(count) for t in range(rows_of // tile)]
    near_count, extra_count = len(near), len(extra)

    def kernel(*refs):
        near_refs, refs = refs[:near_count], refs[near_count:]
        extra_refs, refs = refs[:extra_count], refs[extra_count:]
        one_refs, two_refs, refs = refs[:count], refs[count : 2 * count], refs[2 * count :]
        *out_refs, one_held, two_held, sems = refs

        def copies(s):
            k, at = steps[s]
            slot = s % 2
            return [
                pltpu.make_async_copy(one_refs[k].at[pl.ds(at, tile)], one_held.at[slot], sems.at[0, slot]),
                pltpu.make_async_copy(two_refs[k].at[pl.ds(at, tile)], two_held.at[slot], sems.at[1, slot]),
            ]

        for copy in copies(0):
            copy.start()
        for s, (k, at) in enumerate(steps):
            if s + 1 < len(steps):
                for copy in copies(s + 1):
                    copy.start()
            for copy in copies(s):
                copy.wait()
            kernel_step(s, k, at, tile, near_refs, extra_refs, one_held.at[s % 2], two_held.at[s % 2], out_refs)

    whole = pl.BlockSpec(memory_space=pltpu.VMEM)
    anywhere = pl.BlockSpec(memory_space=pl.ANY)
    dtype = first[0].dtype
    return pl.pallas_call(
        kernel,
        in_specs=[whole] * (near_count + extra_count) + [anywhere] * (2 * count),
        out_specs=[whole] * len(outs),
        out_shape=outs,
        scratch_shapes=[
            pltpu.VMEM((2, tile, width), dtype),
            pltpu.VMEM((2, tile, width), dtype),
            pltpu.SemaphoreType.DMA((2, 2)),
        ],
        compiler_params=pltpu.CompilerParams(vmem_limit_bytes=40 * 1024 * 1024),
        cost_estimate=hint(10.0),
        name=name,
    )(*near, *extra, *first, *second)


def feed_forward(rows_low, inner, outer, bias):
    count, (each, width), rows = len(inner), inner[0].shape, rows_low.shape[0]

    def step(s, k, at, tile, near, extra, inner_tile, outer_tile, outs):
        act, slope = gelu_and_slope(
            dot_nt(near[0][...], inner_tile[...]) + extra[0][pl.ds(k, 1), pl.ds(at, tile)]
        )
        outs[1 + k][:, pl.ds(at, tile)] = act
        outs[1 + count + k][:, pl.ds(at, tile)] = slope
        part = dot_nn(act, outer_tile[...])
        outs[0][...] = part if s == 0 else outs[0][...] + part

    shapes = [jax.ShapeDtypeStruct((rows, width), F32)] + [jax.ShapeDtypeStruct((rows, each), BF)] * (2 * count)
    total, *rest = streamed(step, [rows_low], inner, outer, [bias], shapes, "feed_forward")
    return total, rest[:count], rest[count:]


def feed_forward_back(grad_low, inner, outer, slopes):
    count, (each, width), rows = len(inner), inner[0].shape, grad_low.shape[0]

    def step(s, k, at, tile, near, extra, outer_tile, inner_tile, outs):
        grad = (dot_nt(near[0][...], outer_tile[...]) * extra[k][:, pl.ds(at, tile)].astype(F32)).astype(BF)
        outs[2 + k][:, pl.ds(at, tile)] = grad
        outs[1][pl.ds(k, 1), pl.ds(at, tile)] = jnp.sum(grad.astype(F32), axis=0, keepdims=True)
        part = dot_nn(grad, inner_tile[...])
        outs[0][...] = part if s == 0 else outs[0][...] + part

    shapes = [jax.ShapeDtypeStruct((rows, width), F32), jax.ShapeDtypeStruct((count, each), F32)]
    shapes += [jax.ShapeDtypeStruct((rows, each), BF)] * count
    total, sums, *grads = streamed(step, [grad_low], outer, inner, list(slopes), shapes, "feed_forward_back")
    return total, sums, grads


def weight_grad(pairs, add=None):
    columns, width = pairs[0][0].shape[1], pairs[0][1].shape[1]
    tile = min(256, columns)

    def kernel(*refs):
        total = None
        for k in range(len(pairs)):
            part = dot_tn(refs[2 * k][...], refs[2 * k + 1][...])
            total = part if total is None else total + part
        if add is not None:
            total = total + refs[2 * len(pairs)][...].astype(F32)
        refs[-1][...] = total.astype(BF)

    block = pl.BlockSpec((tile, width), lambda t: (t, 0))
    specs, operands = [], []
    for left, right in pairs:
        specs += [
            pl.BlockSpec((left.shape[0], tile), lambda t: (0, t)),
            pl.BlockSpec(right.shape, lambda t: (0, 0)),
        ]
        operands += [left, right]
    if add is not None:
        specs.append(block)
        operands.append(add)
    return pl.pallas_call(
        kernel,
        grid=(columns // tile,),
        in_specs=specs,
        out_specs=block,
        out_shape=jax.ShapeDtypeStruct((columns, width), BF),
        compiler_params=pltpu.CompilerParams(vmem_limit_bytes=32 * 1024 * 1024),
        cost_estimate=hint(2.0 * sum(a.shape[0] for a, _ in pairs) * columns / (512 * 1024)),
        name="weight_grad",
    )(*operands)


def gradients_out(turned, plain):
    layers, width = len(turned[0]), turned[0][0].shape[1]
    steps = 4

    def kernel(*refs):
        outs = refs[layers * (len(turned) + len(plain)) :]
        for k, out in enumerate(outs):
            for l in range(layers):
                value = refs[k * layers + l][...].astype(F32)
                out[l] = value.T if k < len(turned) else value

    specs, shapes, out_specs = [], [], []
    for arrays in turned:
        rows = arrays[0].shape[0]
        specs += [pl.BlockSpec((rows, width // steps), lambda t: (0, t))] * layers
        out_specs.append(pl.BlockSpec((layers, width // steps, rows), lambda t: (0, t, 0)))
        shapes.append(jax.ShapeDtypeStruct((layers, width, rows), F32))
    for arrays in plain:
        rows = arrays[0].shape[0]
        specs += [pl.BlockSpec((rows // steps, width), lambda t: (t, 0))] * layers
        out_specs.append(pl.BlockSpec((layers, rows // steps, width), lambda t: (0, t, 0)))
        shapes.append(jax.ShapeDtypeStruct((layers, rows, width), F32))
    return pl.pallas_call(
        kernel,
        grid=(steps,),
        in_specs=specs,
        out_specs=out_specs,
        out_shape=shapes,
        compiler_params=pltpu.CompilerParams(vmem_limit_bytes=40 * 1024 * 1024),
        cost_estimate=hint(5.0),
        name="gradients_out",
    )(*[a for arrays in turned + plain for a in arrays])


class Grid:
    def __init__(self, mesh):
        self.nd, self.nt = mesh.shape["dp"], mesh.shape["tensor"]
        self.nx = self.nd // 2

    def place(self):
        self.dp, self.tensor = lax.axis_index("dp"), lax.axis_index("tensor")
        self.x, self.c = self.dp // 2, self.dp % 2

    def swap(self, array, axis, bit):
        count = self.nd if axis == "dp" else self.nt
        return lax.ppermute(array, axis, [(i, i ^ bit) for i in range(count)])

    def core(self, array):
        return self.swap(array, "dp", 1)

    def bits(self, name):
        low, high = {"x": (2, self.nd), "t": (1, self.nt)}[name]
        found = []
        while low < high:
            found.append(low)
            low *= 2
        return found

    def shift(self, array, by, group):
        pairs = [(i, i + by) for i in range(self.nt) if 0 <= i + by < self.nt and i // group == (i + by) // group]
        return lax.ppermute(array, "tensor", pairs)

    def turned(self, array, name, axis):
        count, at = {"x": (self.nx, self.x), "c": (2, self.c), "t": (self.nt, self.tensor)}[name]
        if count == 2:
            return jnp.where(at == 0, array, lax.rev(array, (axis,)))
        return jnp.take(array, at ^ jnp.arange(count), axis=axis)


def together(*values):
    return lax.optimization_barrier(values)


def shards(
    grid,
    inputs,
    segments,
    query_weight,
    query_bias,
    key_weight,
    value_weight,
    value_bias,
    out_weight,
    out_bias,
    first_gain,
    first_shift,
    inner_weight,
    inner_bias,
    outer_weight,
    outer_bias,
    second_gain,
    second_shift,
    cotangent,
):
    g = grid
    g.place()
    layers = query_weight.shape[0]
    rows, width = inputs.shape
    heads = query_weight.shape[2]
    cores = 2 if heads // 2 % HD == 0 else 1
    part = heads // cores
    units = inner_weight.shape[2]
    block = units // g.nd
    length = segments.shape[1]
    group = length // rows
    halo = WINDOW // 2
    high_to_low = g.bits("t")[::-1]

    own = segments[g.tensor // group] if segments.shape[0] > 1 else segments[0]
    spot = g.tensor % group
    seg_q = lax.dynamic_slice(own, (spot * rows,), (rows,))[:, None]
    padded = jnp.pad(own, (halo, halo), constant_values=-1)
    seg_near = lax.dynamic_slice(padded, (spot * rows,), (rows + 2 * halo,))[None]
    seg_far = jnp.take(own.reshape(group, rows), spot ^ jnp.arange(group), axis=0).reshape(1, length)

    def far_rows(array, other=None):
        bit = 1
        while bit < group:
            if other is None:
                other = g.swap(array, "tensor", bit)
            array, other = jnp.concatenate([array, other]), None
            bit *= 2
        return array

    def far_sums(array):
        bit = group // 2
        while bit:
            keep, give = jnp.split(array, 2)
            array = keep.astype(F32) + g.swap(give.astype(BF), "tensor", bit).astype(F32)
            bit //= 2
        return array

    def near_rows(array):
        return jnp.concatenate(
            [g.shift(array[rows - halo :], 1, group), array, g.shift(array[:halo], -1, group)]
        )

    def near_sums(array):
        after_rows = g.shift(array[:halo], -1, group).astype(F32)
        before_rows = g.shift(array[rows + halo :], 1, group).astype(F32)
        edge = jnp.zeros((rows - halo, width), F32)
        return (
            array[halo : rows + halo].astype(F32)
            + jnp.concatenate([edge, after_rows])
            + jnp.concatenate([before_rows, edge])
        )

    step_order = [0]
    for bit in high_to_low:
        step_order = step_order + [m | bit for m in step_order]
    blocks = 2 * g.nx

    def by_steps(array):
        for bit in high_to_low:
            array = jnp.concatenate([array, g.swap(array, "tensor", bit)])
        return array

    def from_steps(array, axis):
        place = jnp.array([step_order.index(m) for m in range(g.nt)])
        return jnp.take(array, place[g.tensor ^ jnp.arange(g.nt)], axis=axis)

    def unit_piece(shard):
        return lax.dynamic_index_in_dim(shard.reshape(g.nd, block, width), g.dp, 0, keepdims=False)

    def over_x(array):
        pieces = [array]
        for bit in g.bits("x"):
            pieces = pieces + [g.swap(a, "dp", bit) for a in pieces]
        return pieces

    def over_core(pieces):
        return pieces + [g.core(a) for a in pieces]

    def head_piece(l):
        pack = jnp.stack([query_weight[l].T, key_weight[l].T, value_weight[l].T, out_weight[l]])
        if cores == 2:
            pack = lax.dynamic_index_in_dim(pack.reshape(4, 2, part, width), g.c, 1, keepdims=False)
        return pack.reshape(1, 4 * part, width)

    def head_first(pack):
        for bit in high_to_low[:-1]:
            pack = jnp.concatenate([pack, g.swap(pack, "tensor", bit)])
        return pack

    def head_last(pack):
        both = [pack, g.swap(pack, "tensor", high_to_low[-1])]
        return [
            jnp.concatenate([a[:, k * part : (k + 1) * part].reshape(-1, width) for a in both]) for k in range(4)
        ]

    def head_rows(kinds):
        return [[a] if cores == 1 else [a, g.core(a)] for a in kinds]

    def bias_rows():
        pack = by_steps(jnp.concatenate([inner_bias, query_bias, value_bias], axis=1)[None])
        unit = pack[..., :units].reshape(g.nt, layers, g.nx, 2, block)
        unit = g.turned(g.turned(unit, "x", 2), "c", 3)
        head = pack[..., units:].reshape(g.nt, layers, 2, cores, part)
        if cores == 2:
            head = g.turned(head, "c", 3)
        unit = jnp.concatenate([unit[:, :1], from_steps(unit[:, 1:], 0)], 1)
        head = jnp.concatenate([head[:, :1], from_steps(head[:, 1:], 0)], 1)
        unit = jnp.transpose(unit, (1, 3, 2, 0, 4)).reshape(layers, blocks, -1)
        return unit, jnp.transpose(head, (1, 2, 3, 0, 4)).reshape(layers, 2, cores, -1)

    moves = [(l, kind) for l in range(layers) for kind in "iu"]
    shard_of = {(l, kind): {"i": inner_weight[l].T, "u": outer_weight[l]}[kind] for l, kind in moves}
    piece_of, gathered, spread, unit_w, head_w = {}, {}, {}, {}, {}
    piece_of[moves[0]] = unit_piece(shard_of[moves[0]])
    stage = 0

    def next_round():
        nonlocal stage
        new = {"piece_of": {}, "gathered": {}, "spread": {}, "unit_w": {}}
        for back, name in enumerate(new):
            if 0 <= stage + 1 - back < len(moves):
                key = moves[stage + 1 - back]
                if back > 1 or key[0] == 0:
                    new[name][key] = (
                        unit_piece(shard_of[key]) if back == 0
                        else by_steps(piece_of[key]) if back == 1
                        else over_x(gathered[key]) if back == 2
                        else over_core(spread[key])
                    )
        stage += 1
        return new

    def end_round(new, carry):
        new, carry = together(new, carry)
        for name, kept in (("piece_of", piece_of), ("gathered", gathered), ("spread", spread), ("unit_w", unit_w)):
            kept.update(new[name])
        return carry

    saved = []
    hidden = inputs.astype(F32)
    new = next_round()
    unit_bias, head_bias = bias_rows()
    far = g.swap(inputs, "tensor", 1) if group > 1 else inputs
    first_part = head_first(head_piece(0))
    later = [
        (jnp.stack([unit_piece(shard_of[l, "i"]), unit_piece(shard_of[l, "u"])]), head_piece(l).reshape(4, part, width))
        for l in range(1, layers)
    ]
    unit_bias, head_bias, far, first_part, later = end_round(new, (unit_bias, head_bias, far, first_part, later))
    for l in range(1, layers):
        both = lax.all_gather(later[l - 1][0], "tensor", axis=0)
        for k, kind in enumerate("iu"):
            gathered[l, kind] = both[:, k].reshape(-1, width)
    new = next_round()
    far_inputs = far_rows(inputs, far)
    kinds = head_last(first_part)
    hidden, far_inputs, kinds, later = end_round(new, (hidden, far_inputs, kinds, later))
    for l in range(layers):
        windowed = l % 2 == 1
        low = hidden.astype(BF)
        new = next_round()
        head_w[l] = head_rows(kinds)
        if l + 1 < layers:
            next_heads = lax.all_gather(later[l][1], "tensor", axis=1).reshape(4, g.nt * part, width)
        if windowed:
            far, seg_k, reach = near_rows(low), seg_near, halo
        else:
            far = far_inputs if l == 0 else far_rows(low)
            seg_k, reach = seg_far, 0
        q_w, k_w, v_w, o_w = head_w[l]
        query = [(dot_nt(low, w) + head_bias[l, 0, k]).astype(BF) for k, w in enumerate(q_w)]
        key = [dot_nt(far, w).astype(BF) for w in k_w]
        value = [(dot_nt(far, w) + head_bias[l, 1, k]).astype(BF) for k, w in enumerate(v_w)]
        context = [attend(*qkv, seg_q, seg_k, reach) for qkv in zip(query, key, value)]
        attended = hidden + out_bias[l]
        for a, w in zip(context, o_w):
            attended = attended + dot_nn(a, w)
        first_normal, first_inverse = norm_stats(attended)
        normed = first_normal * first_gain[l] + first_shift[l]
        normed_low = normed.astype(BF)
        normed, normed_low = end_round(new, (normed, normed_low))
        new = next_round()
        if l + 1 < layers:
            kinds = [next_heads[k] for k in range(4)]
        outer_now = new["unit_w"].get((l, "u"), unit_w.get((l, "u")))
        total, acts, slopes = feed_forward(normed_low, unit_w[l, "i"], outer_now, unit_bias[l])
        mixed = normed + outer_bias[l] + total
        second_normal, second_inverse = norm_stats(mixed)
        hidden = second_normal * second_gain[l] + second_shift[l]
        if l + 1 < layers:
            hidden, acts = end_round(new, (hidden, acts))
        else:
            end_round(new, ())
        swapped = [g.core(a) for a in [normed_low] + acts[g.nx :]]
        saved.append(
            (low, far, query, key, value, seg_k, reach, context, first_normal, first_inverse,
             normed_low, acts, slopes, second_normal, second_inverse, swapped)
        )
    result = hidden

    def unit_parts(mine, others, right):
        return [weight_grad(list(zip(both, right))) for both in zip(mine, others)]

    def sum_over_x(parts):
        for bit in g.bits("x")[::-1]:
            keep, give = parts[: len(parts) // 2], parts[len(parts) // 2 :]
            parts = [(a.astype(F32) + g.swap(b, "dp", bit).astype(F32)).astype(BF) for a, b in zip(keep, give)]
        return parts[0]

    def head_total(lefts, right):
        received = g.core(weight_grad([(lefts[1], right)])) if cores == 2 else None
        return weight_grad([(lefts[0], right)], received).reshape(g.nt, part, width)

    def one_step(total, bit):
        keep, give = jnp.split(total, 2)
        return (keep.astype(F32) + g.swap(give, "tensor", bit).astype(F32)).astype(BF)

    def end_over_x(wide, plain, total):
        wide = wide[None]
        for bit in g.bits("x"):
            wide = jnp.concatenate([wide, g.swap(wide, "dp", bit)])
            if plain is not None:
                plain = (plain.astype(F32) + g.swap(plain, "dp", bit).astype(F32)).astype(BF)
            total = (total.astype(F32) + g.swap(total, "dp", bit).astype(F32)).astype(BF)
        return wide, plain, total

    def end_over_core(wide, plain, total):
        wide = jnp.stack([wide, g.core(wide)], 1)
        wide = g.turned(g.turned(wide, "x", 0), "c", 1)
        if plain is not None:
            plain = jnp.stack([plain, g.core(plain)]).reshape(2, g.nx, block, width)
            plain = g.turned(plain, "c", 0).swapaxes(0, 1)
        if cores == 2:
            return wide, plain, g.turned(jnp.stack([total, g.core(total)]), "c", 0)
        return wide, plain, (total.astype(F32) + g.core(total).astype(F32))[None]

    ends, vectors = [None] * layers, [None] * layers
    later_sums, later_outer = [None] * layers, [None] * layers

    def over_tensor(arrays):
        pack = jnp.concatenate(arrays, 1).reshape(-1, width)
        return lax.psum_scatter(pack, "tensor", scatter_dimension=0, tiled=True)

    grad_hidden = cotangent.astype(F32)
    units_before = None
    first_bits = high_to_low[::-1]
    for l in reversed(range(layers)):
        (low, far, query, key, value, seg_k, reach, context, first_normal, first_inverse,
         normed_low, acts, slopes, second_normal, second_inverse, swapped) = saved[l]
        q_w, k_w, v_w, o_w = head_w[l]
        inner_w, outer_w = unit_w[l, "i"], unit_w[l, "u"]
        grad_mixed, d_second_gain, d_second_shift = norm_back(
            grad_hidden, second_normal, second_inverse, second_gain[l]
        )
        mixed_low = grad_mixed.astype(BF)
        d_outer_bias = jnp.sum(grad_mixed, axis=0)
        mixed_both = mixed_low, g.core(mixed_low)
        normed_both = normed_low, swapped[0]
        outer_parts = unit_parts(acts[: g.nx], swapped[1:], mixed_both)
        outer_parts, mixed_low, grad_mixed, units_before = together(
            outer_parts, mixed_low, grad_mixed, units_before
        )
        if units_before is not None:
            later_sums[l + 1] = over_tensor(units_before)
        if l:
            later_outer[l] = over_tensor([a.reshape(g.nt, block, width) for a in outer_parts])
            outer_sum = None
        else:
            outer_sum = sum_over_x(outer_parts).reshape(g.nt, block, width)
        total, d_inner_bias, grad_inner = feed_forward_back(mixed_low, inner_w, outer_w, slopes)
        inner_parts = unit_parts(grad_inner[: g.nx], [g.core(a) for a in grad_inner[g.nx :]], normed_both)
        grad_normed = grad_mixed + total
        grad_attended, d_first_gain, d_first_shift = norm_back(
            grad_normed, first_normal, first_inverse, first_gain[l]
        )
        inner_parts, grad_attended = together(inner_parts, grad_attended)
        inner_sum = sum_over_x(inner_parts).reshape(g.nt, block, width)
        d_out_bias = jnp.sum(grad_attended, axis=0)
        attended_low = grad_attended.astype(BF)
        grad_context = [dot_nt(attended_low, w).astype(BF) for w in o_w]
        out_total = head_total(context, attended_low)
        backs = []
        for k in range(cores):
            backs.append(attend_back(query[k], key[k], value[k], grad_context[k], seg_q, seg_k, reach))
            if k == 0:
                backs, outer_sum, grad_context, out_total = together(backs, outer_sum, grad_context, out_total)
            elif l == 0:
                outer_sum, out_total = one_step(outer_sum, first_bits[0]), one_step(out_total, first_bits[0])
        backs, outer_sum, out_total = together(backs, outer_sum, out_total)
        d_query, d_key, d_value = zip(*backs)
        far_part = sum(
            dot_nn(a, w) for grad, weight in ((d_key, k_w), (d_value, v_w)) for a, w in zip(grad, weight)
        ).astype(BF)
        near_sum = grad_attended
        for a, w in zip(d_query, q_w):
            near_sum = near_sum + dot_nn(a, w)
        v_total = head_total(d_value, far)
        totals = [head_total(d_query, low), head_total(d_key, far), v_total]
        unit_order = d_inner_bias.reshape(2, g.nx, g.nt, block)
        unit_order = g.turned(g.turned(unit_order, "c", 0), "x", 1)
        if l == 0:
            unit_order = from_steps(unit_order, 2)
        head_grad = jnp.stack(
            [jnp.stack([jnp.sum(a, axis=0, dtype=F32) for a in grad]) for grad in (d_query, d_value)]
        ).reshape(2, cores, g.nt, part)
        if cores == 2:
            head_grad = g.turned(head_grad, "c", 1)
        if l == 0:
            head_grad = from_steps(head_grad, 2)
        vectors[l] = jnp.concatenate(
            [d_out_bias, d_first_gain, d_first_shift, d_outer_bias, d_second_gain, d_second_shift,
             jnp.transpose(unit_order, (2, 1, 0, 3)).reshape(-1),
             jnp.transpose(head_grad, (0, 2, 1, 3)).reshape(-1)]
        )
        if l:
            far_sum = near_sums(far_part) if reach else far_sums(far_part)
            grad_hidden = near_sum + far_sum
            units_before = [inner_sum, *totals, out_total]
    steps_done = cores - 1
    vector = jnp.stack(vectors)
    hops = [(axis, 1 << k) for axis, count in (("dp", g.nd), ("tensor", g.nt)) for k in range(count.bit_length() - 1)]
    far_bits = [1 << k for k in range(group.bit_length() - 1)][::-1]

    def next_hop(vector):
        return vector + g.swap(vector, *hops.pop(0)) if hops else vector

    for bit in first_bits[steps_done : steps_done + 1]:
        outer_sum, out_total = one_step(outer_sum, bit), one_step(out_total, bit)
    inner_sum, totals[2] = one_step(inner_sum, first_bits[0]), one_step(totals[2], first_bits[0])
    totals, outer_sum, out_total, inner_sum, vector, far_part = together(
        totals, outer_sum, out_total, inner_sum, vector, far_part
    )
    for number, bit in enumerate(first_bits):
        totals[:2] = [one_step(a, bit) for a in totals[:2]]
        if number + 1 < len(first_bits):
            inner_sum = one_step(inner_sum, first_bits[number + 1])
            totals[2] = one_step(totals[2], first_bits[number + 1])
        if number + steps_done + 1 < len(first_bits):
            more = first_bits[number + steps_done + 1]
            outer_sum, out_total = one_step(outer_sum, more), one_step(out_total, more)
        vector = next_hop(vector)
        if far_bits:
            keep, give = jnp.split(far_part, 2)
            far_part = keep.astype(F32) + g.swap(give.astype(BF), "tensor", far_bits.pop(0)).astype(F32)
        if number == 1:
            for l in range(1, layers):
                plain = g.turned(later_outer[l].reshape(-1, block, width), "x", 0).reshape(-1, width)
                ends[l] = end_over_x(later_sums[l][:block], plain, later_sums[l][block:])
        if number == 2:
            for l in range(1, layers):
                ends[l] = end_over_core(*ends[l])
        totals, outer_sum, out_total, inner_sum, vector, far_part, ends = together(
            totals, outer_sum, out_total, inner_sum, vector, far_part, ends
        )
    while far_bits:
        keep, give = jnp.split(far_part, 2)
        far_part = keep.astype(F32) + g.swap(give.astype(BF), "tensor", far_bits.pop(0)).astype(F32)
    grad_hidden = near_sum + far_part
    wide = jnp.concatenate([a.reshape(-1, width) for a in (inner_sum, outer_sum)])
    total = jnp.concatenate([a.reshape(-1, width) for a in (*totals, out_total)])
    vector = next_hop(vector)
    wide, _, total = end_over_x(wide, None, total)
    wide, total, vector = together(wide, total, vector)
    ends[0] = end_over_core(wide, None, total)
    while hops:
        vector = next_hop(vector)

    shared = [vector[:, k * width : (k + 1) * width] for k in range(6)]

    def own_part(start, count):
        return lax.dynamic_slice(vector, (0, start + g.tensor * count), (layers, count))

    d_inner_bias = own_part(6 * width, units)
    d_query_bias = own_part(6 * width + units * g.nt, heads)
    d_value_bias = own_part(6 * width + (units + heads) * g.nt, heads)

    def shard(l, kind):
        wide, plain, total = ends[l]
        if kind == "u" and plain is not None:
            array = plain.reshape(units, width)
        elif kind in "iu":
            k = "iu".index(kind)
            array = wide[:, :, k * block : (k + 1) * block].reshape(units, width)
        else:
            k = "qkvo".index(kind)
            array = total[:, k * part : (k + 1) * part].reshape(heads, width)
        return array

    kinds = [[shard(l, kind) for l in range(layers)] for kind in "qkviou"]
    d_query, d_key, d_value, d_inner, d_out, d_outer = gradients_out(kinds[:4], kinds[4:])
    return (
        result,
        grad_hidden,
        d_query,
        d_query_bias,
        d_key,
        d_value,
        d_value_bias,
        d_out,
        shared[0],
        shared[1],
        shared[2],
        d_inner,
        d_inner_bias,
        d_outer,
        shared[3],
        shared[4],
        shared[5],
    )


def solution(mesh):
    rows = P(("dp", "tensor"), None)
    columns = P(None, None, "tensor")
    units = P(None, "tensor", None)
    vector = P(None, "tensor")
    in_specs = (
        rows, P("dp", None), columns, vector, columns, columns, vector, units, P(), P(), P(),
        columns, vector, units, P(), P(), P(), rows,
    )
    out_specs = (
        rows, rows, columns, vector, columns, columns, vector, units, P(), P(), P(),
        columns, vector, units, P(), P(), P(),
    )
    return jax.shard_map(
        partial(shards, Grid(mesh)), mesh=mesh, in_specs=in_specs, out_specs=out_specs, check_vma=False
    )
```

```python
from functools import partial

import jax
import jax.numpy as jnp
from jax import lax
from jax.experimental import pallas as pl
from jax.experimental.pallas import tpu as pltpu
from jax.sharding import PartitionSpec as P

HD = 64
WINDOW = 256
EPS = 1e-05
NEGATIVE = -1e30
BF = jnp.bfloat16
F32 = jnp.float32
LANES = 128


def dot_nn(left, right):
    return lax.dot_general(left, right, (((1,), (0,)), ((), ())), preferred_element_type=F32)


def dot_nt(left, right):
    return lax.dot_general(left, right, (((1,), (1,)), ((), ())), preferred_element_type=F32)


def dot_tn(left, right):
    return lax.dot_general(left, right, (((0,), (0,)), ((), ())), preferred_element_type=F32)


def allowed_keys(seg_q, seg_k, halo):
    allowed = seg_q == seg_k
    if halo:
        row = lax.broadcasted_iota(jnp.int32, allowed.shape, 0)
        col = lax.broadcasted_iota(jnp.int32, allowed.shape, 1)
        allowed = jnp.logical_and(allowed, jnp.abs(row + halo - col) <= WINDOW // 2)
    return allowed


def head_lanes(shape, head):
    lane = lax.broadcasted_iota(jnp.int32, shape, 1)
    return (lane // HD) == head


def probabilities(query, key, allowed):
    scores = jnp.where(allowed, dot_nt(query, key) * (HD ** -0.5), NEGATIVE)
    raised = jnp.exp(scores - jnp.max(scores, axis=-1, keepdims=True))
    return raised * (1.0 / jnp.sum(raised, axis=-1, keepdims=True))


def attend_kernel(halo, seg_q_ref, seg_k_ref, q_ref, k_ref, v_ref, c_ref):
    allowed = allowed_keys(seg_q_ref[...], seg_k_ref[...], halo)
    query, key, value = q_ref[...], k_ref[...], v_ref[...]
    total = None
    for head in range(LANES // HD):
        mine = head_lanes(query.shape, head)
        probs = probabilities(jnp.where(mine, query, jnp.zeros_like(query)), key, allowed)
        part = jnp.where(mine, dot_nn(probs.astype(BF), value), 0.0)
        total = part if total is None else total + part
    c_ref[...] = total.astype(BF)


def attend_back_kernel(halo, seg_q_ref, seg_k_ref, q_ref, k_ref, v_ref, g_ref, dq_ref, dk_ref, dv_ref):
    allowed = allowed_keys(seg_q_ref[...], seg_k_ref[...], halo)
    query, key, value, grad = q_ref[...], k_ref[...], v_ref[...], g_ref[...]
    dq = dk = dv = None
    for head in range(LANES // HD):
        mine = head_lanes(query.shape, head)
        own_q = jnp.where(mine, query, jnp.zeros_like(query))
        own_g = jnp.where(mine, grad, jnp.zeros_like(grad))
        probs = probabilities(own_q, key, allowed)
        grad_probs = dot_nt(own_g, value)
        delta = jnp.sum(probs * grad_probs, axis=-1, keepdims=True)
        grad_scores = (probs * (grad_probs - delta)).astype(BF)
        q_part = jnp.where(mine, dot_nn(grad_scores, key), 0.0)
        k_part = dot_tn(grad_scores, own_q)
        v_part = dot_tn(probs.astype(BF), own_g)
        dq = q_part if dq is None else dq + q_part
        dk = k_part if dk is None else dk + k_part
        dv = v_part if dv is None else dv + v_part
    dq_ref[...] = (dq * (HD ** -0.5)).astype(BF)
    dk_ref[...] = (dk * (HD ** -0.5)).astype(BF)
    dv_ref[...] = dv.astype(BF)


def attend(query, key, value, seg_q, seg_k, halo):
    rows, width = query.shape
    keys = key.shape[0]
    whole = lambda shape: pl.BlockSpec(shape, lambda p: (0, 0))
    near = pl.BlockSpec((rows, LANES), lambda p: (0, p))
    far = pl.BlockSpec((keys, LANES), lambda p: (0, p))
    return pl.pallas_call(
        partial(attend_kernel, halo),
        grid=(width // LANES,),
        in_specs=[whole((rows, 1)), whole((1, keys)), near, far, far],
        out_specs=near,
        out_shape=jax.ShapeDtypeStruct((rows, width), BF),
        compiler_params=pltpu.CompilerParams(vmem_limit_bytes=40 * 1024 * 1024),
        cost_estimate=hint(6.5 * keys / 1024),
        name="attend",
    )(seg_q, seg_k, query, key, value)


def attend_back(query, key, value, grad, seg_q, seg_k, halo):
    rows, width = query.shape
    keys = key.shape[0]
    whole = lambda shape: pl.BlockSpec(shape, lambda p: (0, 0))
    near = pl.BlockSpec((rows, LANES), lambda p: (0, p))
    far = pl.BlockSpec((keys, LANES), lambda p: (0, p))
    return pl.pallas_call(
        partial(attend_back_kernel, halo),
        grid=(width // LANES,),
        in_specs=[whole((rows, 1)), whole((1, keys)), near, far, far, near],
        out_specs=[near, far, far],
        out_shape=[
            jax.ShapeDtypeStruct((rows, width), BF),
            jax.ShapeDtypeStruct((keys, width), BF),
            jax.ShapeDtypeStruct((keys, width), BF),
        ],
        compiler_params=pltpu.CompilerParams(vmem_limit_bytes=48 * 1024 * 1024),
        cost_estimate=hint(10.0 * keys / 1024),
        name="attend_back",
    )(seg_q, seg_k, query, key, value, grad)


def norm_stats(values):
    center = values - jnp.mean(values, axis=-1, keepdims=True)
    inverse = lax.rsqrt(jnp.mean(center * center, axis=-1, keepdims=True) + EPS)
    return center * inverse, inverse


def norm_back(grad, normal, inverse, gain):
    scaled = grad * gain
    back = inverse * (
        scaled
        - jnp.mean(scaled, axis=-1, keepdims=True)
        - normal * jnp.mean(scaled * normal, axis=-1, keepdims=True)
    )
    return back, jnp.sum(grad * normal, axis=0), jnp.sum(grad, axis=0)


def gelu_and_slope(inner):
    half = 0.5 * (1.0 + lax.erf(inner * (0.5 ** 0.5)))
    bell = jnp.exp(-0.5 * inner * inner) * ((2.0 * jnp.pi) ** -0.5)
    return (inner * half).astype(BF), (half + inner * bell).astype(BF)


def hint(us):
    return pl.CostEstimate(flops=0, bytes_accessed=int(us * 1.3e6), transcendentals=0)


def streamed(kernel_step, near, first, second, extra, outs, name):
    count, (rows_of, width) = len(first), first[0].shape
    tile = min(512, rows_of)
    steps = [(k, t * tile) for k in range(count) for t in range(rows_of // tile)]
    near_count, extra_count = len(near), len(extra)

    def kernel(*refs):
        near_refs, refs = refs[:near_count], refs[near_count:]
        extra_refs, refs = refs[:extra_count], refs[extra_count:]
        one_refs, two_refs, refs = refs[:count], refs[count : 2 * count], refs[2 * count :]
        *out_refs, one_held, two_held, sems = refs

        def copies(s):
            k, at = steps[s]
            slot = s % 2
            return [
                pltpu.make_async_copy(one_refs[k].at[pl.ds(at, tile)], one_held.at[slot], sems.at[0, slot]),
                pltpu.make_async_copy(two_refs[k].at[pl.ds(at, tile)], two_held.at[slot], sems.at[1, slot]),
            ]

        for copy in copies(0):
            copy.start()
        for s, (k, at) in enumerate(steps):
            if s + 1 < len(steps):
                for copy in copies(s + 1):
                    copy.start()
            for copy in copies(s):
                copy.wait()
            kernel_step(s, k, at, tile, near_refs, extra_refs, one_held.at[s % 2], two_held.at[s % 2], out_refs)

    whole = pl.BlockSpec(memory_space=pltpu.VMEM)
    anywhere = pl.BlockSpec(memory_space=pl.ANY)
    dtype = first[0].dtype
    return pl.pallas_call(
        kernel,
        in_specs=[whole] * (near_count + extra_count) + [anywhere] * (2 * count),
        out_specs=[whole] * len(outs),
        out_shape=outs,
        scratch_shapes=[
            pltpu.VMEM((2, tile, width), dtype),
            pltpu.VMEM((2, tile, width), dtype),
            pltpu.SemaphoreType.DMA((2, 2)),
        ],
        compiler_params=pltpu.CompilerParams(vmem_limit_bytes=40 * 1024 * 1024),
        cost_estimate=hint(10.0),
        name=name,
    )(*near, *extra, *first, *second)


def feed_forward(rows_low, inner, outer, bias):
    count, (each, width), rows = len(inner), inner[0].shape, rows_low.shape[0]

    def step(s, k, at, tile, near, extra, inner_tile, outer_tile, outs):
        act, slope = gelu_and_slope(
            dot_nt(near[0][...], inner_tile[...]) + extra[0][pl.ds(k, 1), pl.ds(at, tile)]
        )
        outs[1 + k][:, pl.ds(at, tile)] = act
        outs[1 + count + k][:, pl.ds(at, tile)] = slope
        part = dot_nn(act, outer_tile[...])
        outs[0][...] = part if s == 0 else outs[0][...] + part

    shapes = [jax.ShapeDtypeStruct((rows, width), F32)] + [jax.ShapeDtypeStruct((rows, each), BF)] * (2 * count)
    total, *rest = streamed(step, [rows_low], inner, outer, [bias], shapes, "feed_forward")
    return total, rest[:count], rest[count:]


def feed_forward_back(grad_low, inner, outer, slopes):
    count, (each, width), rows = len(inner), inner[0].shape, grad_low.shape[0]

    def step(s, k, at, tile, near, extra, outer_tile, inner_tile, outs):
        grad = (dot_nt(near[0][...], outer_tile[...]) * extra[k][:, pl.ds(at, tile)].astype(F32)).astype(BF)
        outs[2 + k][:, pl.ds(at, tile)] = grad
        outs[1][pl.ds(k, 1), pl.ds(at, tile)] = jnp.sum(grad.astype(F32), axis=0, keepdims=True)
        part = dot_nn(grad, inner_tile[...])
        outs[0][...] = part if s == 0 else outs[0][...] + part

    shapes = [jax.ShapeDtypeStruct((rows, width), F32), jax.ShapeDtypeStruct((count, each), F32)]
    shapes += [jax.ShapeDtypeStruct((rows, each), BF)] * count
    total, sums, *grads = streamed(step, [grad_low], outer, inner, list(slopes), shapes, "feed_forward_back")
    return total, sums, grads


def weight_grad(pairs, add=None):
    columns, width = pairs[0][0].shape[1], pairs[0][1].shape[1]
    tile = min(256, columns)

    def kernel(*refs):
        total = None
        for k in range(len(pairs)):
            part = dot_tn(refs[2 * k][...], refs[2 * k + 1][...])
            total = part if total is None else total + part
        if add is not None:
            total = total + refs[2 * len(pairs)][...].astype(F32)
        refs[-1][...] = total.astype(BF)

    block = pl.BlockSpec((tile, width), lambda t: (t, 0))
    specs, operands = [], []
    for left, right in pairs:
        specs += [
            pl.BlockSpec((left.shape[0], tile), lambda t: (0, t)),
            pl.BlockSpec(right.shape, lambda t: (0, 0)),
        ]
        operands += [left, right]
    if add is not None:
        specs.append(block)
        operands.append(add)
    return pl.pallas_call(
        kernel,
        grid=(columns // tile,),
        in_specs=specs,
        out_specs=block,
        out_shape=jax.ShapeDtypeStruct((columns, width), BF),
        compiler_params=pltpu.CompilerParams(vmem_limit_bytes=32 * 1024 * 1024),
        cost_estimate=hint(2.0 * sum(a.shape[0] for a, _ in pairs) * columns / (512 * 1024)),
        name="weight_grad",
    )(*operands)


def gradients_out(turned, plain):
    layers, width = len(turned[0]), turned[0][0].shape[1]
    steps = 4

    def kernel(*refs):
        outs = refs[layers * (len(turned) + len(plain)) :]
        for k, out in enumerate(outs):
            for l in range(layers):
                value = refs[k * layers + l][...].astype(F32)
                out[l] = value.T if k < len(turned) else value

    specs, shapes, out_specs = [], [], []
    for arrays in turned:
        rows = arrays[0].shape[0]
        specs += [pl.BlockSpec((rows, width // steps), lambda t: (0, t))] * layers
        out_specs.append(pl.BlockSpec((layers, width // steps, rows), lambda t: (0, t, 0)))
        shapes.append(jax.ShapeDtypeStruct((layers, width, rows), F32))
    for arrays in plain:
        rows = arrays[0].shape[0]
        specs += [pl.BlockSpec((rows // steps, width), lambda t: (t, 0))] * layers
        out_specs.append(pl.BlockSpec((layers, rows // steps, width), lambda t: (0, t, 0)))
        shapes.append(jax.ShapeDtypeStruct((layers, rows, width), F32))
    return pl.pallas_call(
        kernel,
        grid=(steps,),
        in_specs=specs,
        out_specs=out_specs,
        out_shape=shapes,
        compiler_params=pltpu.CompilerParams(vmem_limit_bytes=40 * 1024 * 1024),
        cost_estimate=hint(5.0),
        name="gradients_out",
    )(*[a for arrays in turned + plain for a in arrays])


class Grid:
    def __init__(self, mesh):
        self.nd, self.nt = mesh.shape["dp"], mesh.shape["tensor"]
        self.nx = self.nd // 2

    def place(self):
        self.dp, self.tensor = lax.axis_index("dp"), lax.axis_index("tensor")
        self.x, self.c = self.dp // 2, self.dp % 2

    def swap(self, array, axis, bit):
        count = self.nd if axis == "dp" else self.nt
        return lax.ppermute(array, axis, [(i, i ^ bit) for i in range(count)])

    def core(self, array):
        return self.swap(array, "dp", 1)

    def bits(self, name):
        low, high = {"x": (2, self.nd), "t": (1, self.nt)}[name]
        found = []
        while low < high:
            found.append(low)
            low *= 2
        return found

    def shift(self, array, by, group):
        pairs = [(i, i + by) for i in range(self.nt) if 0 <= i + by < self.nt and i // group == (i + by) // group]
        return lax.ppermute(array, "tensor", pairs)

    def turned(self, array, name, axis):
        count, at = {"x": (self.nx, self.x), "c": (2, self.c), "t": (self.nt, self.tensor)}[name]
        if count == 2:
            return jnp.where(at == 0, array, lax.rev(array, (axis,)))
        return jnp.take(array, at ^ jnp.arange(count), axis=axis)


def together(*values):
    return lax.optimization_barrier(values)


def shards(
    grid,
    inputs,
    segments,
    query_weight,
    query_bias,
    key_weight,
    value_weight,
    value_bias,
    out_weight,
    out_bias,
    first_gain,
    first_shift,
    inner_weight,
    inner_bias,
    outer_weight,
    outer_bias,
    second_gain,
    second_shift,
    cotangent,
):
    g = grid
    g.place()
    layers = query_weight.shape[0]
    rows, width = inputs.shape
    heads = query_weight.shape[2]
    cores = 2 if heads // 2 % HD == 0 else 1
    part = heads // cores
    units = inner_weight.shape[2]
    block = units // g.nd
    length = segments.shape[1]
    group = length // rows
    halo = WINDOW // 2
    high_to_low = g.bits("t")[::-1]

    own = segments[g.tensor // group] if segments.shape[0] > 1 else segments[0]
    spot = g.tensor % group
    seg_q = lax.dynamic_slice(own, (spot * rows,), (rows,))[:, None]
    padded = jnp.pad(own, (halo, halo), constant_values=-1)
    seg_near = lax.dynamic_slice(padded, (spot * rows,), (rows + 2 * halo,))[None]
    seg_far = jnp.take(own.reshape(group, rows), spot ^ jnp.arange(group), axis=0).reshape(1, length)

    def far_rows(array, other=None):
        bit = 1
        while bit < group:
            if other is None:
                other = g.swap(array, "tensor", bit)
            array, other = jnp.concatenate([array, other]), None
            bit *= 2
        return array

    def far_sums(array):
        bit = group // 2
        while bit:
            keep, give = jnp.split(array, 2)
            array = keep.astype(F32) + g.swap(give.astype(BF), "tensor", bit).astype(F32)
            bit //= 2
        return array

    def near_rows(array):
        return jnp.concatenate(
            [g.shift(array[rows - halo :], 1, group), array, g.shift(array[:halo], -1, group)]
        )

    def near_sums(array):
        after_rows = g.shift(array[:halo], -1, group).astype(F32)
        before_rows = g.shift(array[rows + halo :], 1, group).astype(F32)
        edge = jnp.zeros((rows - halo, width), F32)
        return (
            array[halo : rows + halo].astype(F32)
            + jnp.concatenate([edge, after_rows])
            + jnp.concatenate([before_rows, edge])
        )

    step_order = [0]
    for bit in high_to_low:
        step_order = step_order + [m | bit for m in step_order]
    blocks = 2 * g.nx

    def by_steps(array):
        for bit in high_to_low:
            array = jnp.concatenate([array, g.swap(array, "tensor", bit)])
        return array

    def from_steps(array, axis):
        place = jnp.array([step_order.index(m) for m in range(g.nt)])
        return jnp.take(array, place[g.tensor ^ jnp.arange(g.nt)], axis=axis)

    def unit_piece(shard):
        return lax.dynamic_index_in_dim(shard.reshape(g.nd, block, width), g.dp, 0, keepdims=False)

    def over_x(array):
        pieces = [array]
        for bit in g.bits("x"):
            pieces = pieces + [g.swap(a, "dp", bit) for a in pieces]
        return pieces

    def over_core(pieces):
        return pieces + [g.core(a) for a in pieces]

    def head_piece(l):
        pack = jnp.stack([query_weight[l].T, key_weight[l].T, value_weight[l].T, out_weight[l]])
        if cores == 2:
            pack = lax.dynamic_index_in_dim(pack.reshape(4, 2, part, width), g.c, 1, keepdims=False)
        return pack.reshape(1, 4 * part, width)

    def head_first(pack):
        for bit in high_to_low[:-1]:
            pack = jnp.concatenate([pack, g.swap(pack, "tensor", bit)])
        return pack

    def head_last(pack):
        both = [pack, g.swap(pack, "tensor", high_to_low[-1])]
        return [
            jnp.concatenate([a[:, k * part : (k + 1) * part].reshape(-1, width) for a in both]) for k in range(4)
        ]

    def head_rows(kinds):
        return [[a] if cores == 1 else [a, g.core(a)] for a in kinds]

    def bias_rows():
        pack = by_steps(jnp.concatenate([inner_bias, query_bias, value_bias], axis=1)[None])
        unit = pack[..., :units].reshape(g.nt, layers, g.nx, 2, block)
        unit = g.turned(g.turned(unit, "x", 2), "c", 3)
        head = pack[..., units:].reshape(g.nt, layers, 2, cores, part)
        if cores == 2:
            head = g.turned(head, "c", 3)
        unit = jnp.concatenate([unit[:, :1], from_steps(unit[:, 1:], 0)], 1)
        head = jnp.concatenate([head[:, :1], from_steps(head[:, 1:], 0)], 1)
        unit = jnp.transpose(unit, (1, 3, 2, 0, 4)).reshape(layers, blocks, -1)
        return unit, jnp.transpose(head, (1, 2, 3, 0, 4)).reshape(layers, 2, cores, -1)

    moves = [(l, kind) for l in range(layers) for kind in "iu"]
    shard_of = {(l, kind): {"i": inner_weight[l].T, "u": outer_weight[l]}[kind] for l, kind in moves}
    piece_of, gathered, spread, unit_w, head_w = {}, {}, {}, {}, {}
    piece_of[moves[0]] = unit_piece(shard_of[moves[0]])
    stage = 0

    def next_round():
        nonlocal stage
        new = {"piece_of": {}, "gathered": {}, "spread": {}, "unit_w": {}}
        for back, name in enumerate(new):
            if 0 <= stage + 1 - back < len(moves):
                key = moves[stage + 1 - back]
                if back > 1 or key[0] == 0:
                    new[name][key] = (
                        unit_piece(shard_of[key]) if back == 0
                        else by_steps(piece_of[key]) if back == 1
                        else over_x(gathered[key]) if back == 2
                        else over_core(spread[key])
                    )
        stage += 1
        return new

    def end_round(new, carry):
        new, carry = together(new, carry)
        for name, kept in (("piece_of", piece_of), ("gathered", gathered), ("spread", spread), ("unit_w", unit_w)):
            kept.update(new[name])
        return carry

    saved = []
    hidden = inputs.astype(F32)
    new = next_round()
    unit_bias, head_bias = bias_rows()
    far = g.swap(inputs, "tensor", 1) if group > 1 else inputs
    first_part = head_first(head_piece(0))
    later = [
        (jnp.stack([unit_piece(shard_of[l, "i"]), unit_piece(shard_of[l, "u"])]), head_piece(l).reshape(4, part, width))
        for l in range(1, layers)
    ]
    unit_bias, head_bias, far, first_part, later = end_round(new, (unit_bias, head_bias, far, first_part, later))
    for l in range(1, layers):
        both = lax.all_gather(later[l - 1][0], "tensor", axis=0)
        for k, kind in enumerate("iu"):
            gathered[l, kind] = both[:, k].reshape(-1, width)
    new = next_round()
    far_inputs = far_rows(inputs, far)
    kinds = head_last(first_part)
    hidden, far_inputs, kinds, later = end_round(new, (hidden, far_inputs, kinds, later))
    for l in range(layers):
        windowed = l % 2 == 1
        low = hidden.astype(BF)
        new = next_round()
        head_w[l] = head_rows(kinds)
        if l + 1 < layers:
            next_heads = lax.all_gather(later[l][1], "tensor", axis=1).reshape(4, g.nt * part, width)
        if windowed:
            far, seg_k, reach = near_rows(low), seg_near, halo
        else:
            far = far_inputs if l == 0 else far_rows(low)
            seg_k, reach = seg_far, 0
        q_w, k_w, v_w, o_w = head_w[l]
        query = [(dot_nt(low, w) + head_bias[l, 0, k]).astype(BF) for k, w in enumerate(q_w)]
        key = [dot_nt(far, w).astype(BF) for w in k_w]
        value = [(dot_nt(far, w) + head_bias[l, 1, k]).astype(BF) for k, w in enumerate(v_w)]
        context = [attend(*qkv, seg_q, seg_k, reach) for qkv in zip(query, key, value)]
        attended = hidden + out_bias[l]
        for a, w in zip(context, o_w):
            attended = attended + dot_nn(a, w)
        first_normal, first_inverse = norm_stats(attended)
        normed = first_normal * first_gain[l] + first_shift[l]
        normed_low = normed.astype(BF)
        normed, normed_low = end_round(new, (normed, normed_low))
        new = next_round()
        if l + 1 < layers:
            kinds = [next_heads[k] for k in range(4)]
        outer_now = new["unit_w"].get((l, "u"), unit_w.get((l, "u")))
        total, acts, slopes = feed_forward(normed_low, unit_w[l, "i"], outer_now, unit_bias[l])
        mixed = normed + outer_bias[l] + total
        second_normal, second_inverse = norm_stats(mixed)
        hidden = second_normal * second_gain[l] + second_shift[l]
        if l + 1 < layers:
            hidden, acts = end_round(new, (hidden, acts))
        else:
            end_round(new, ())
        swapped = [g.core(a) for a in [normed_low] + acts[g.nx :]]
        saved.append(
            (low, far, query, key, value, seg_k, reach, context, first_normal, first_inverse,
             normed_low, acts, slopes, second_normal, second_inverse, swapped)
        )
    result = hidden

    def unit_parts(mine, others, right):
        return [weight_grad(list(zip(both, right))) for both in zip(mine, others)]

    def sum_over_x(parts):
        for bit in g.bits("x")[::-1]:
            keep, give = parts[: len(parts) // 2], parts[len(parts) // 2 :]
            parts = [(a.astype(F32) + g.swap(b, "dp", bit).astype(F32)).astype(BF) for a, b in zip(keep, give)]
        return parts[0]

    def head_total(lefts, right):
        received = g.core(weight_grad([(lefts[1], right)])) if cores == 2 else None
        return weight_grad([(lefts[0], right)], received).reshape(g.nt, part, width)

    def one_step(total, bit):
        keep, give = jnp.split(total, 2)
        return (keep.astype(F32) + g.swap(give, "tensor", bit).astype(F32)).astype(BF)

    def end_over_x(wide, plain, total):
        wide = wide[None]
        for bit in g.bits("x"):
            wide = jnp.concatenate([wide, g.swap(wide, "dp", bit)])
            if plain is not None:
                plain = (plain.astype(F32) + g.swap(plain, "dp", bit).astype(F32)).astype(BF)
            total = (total.astype(F32) + g.swap(total, "dp", bit).astype(F32)).astype(BF)
        return wide, plain, total

    def end_over_core(wide, plain, total):
        wide = jnp.stack([wide, g.core(wide)], 1)
        wide = g.turned(g.turned(wide, "x", 0), "c", 1)
        if plain is not None:
            plain = jnp.stack([plain, g.core(plain)]).reshape(2, g.nx, block, width)
            plain = g.turned(plain, "c", 0).swapaxes(0, 1)
        if cores == 2:
            return wide, plain, g.turned(jnp.stack([total, g.core(total)]), "c", 0)
        return wide, plain, (total.astype(F32) + g.core(total).astype(F32))[None]

    ends, vectors = [None] * layers, [None] * layers
    later_sums, later_outer = [None] * layers, [None] * layers

    def over_tensor(arrays):
        pack = jnp.concatenate(arrays, 1).reshape(-1, width)
        return lax.psum_scatter(pack, "tensor", scatter_dimension=0, tiled=True)

    grad_hidden = cotangent.astype(F32)
    units_before = None
    first_bits = high_to_low[::-1]
    for l in reversed(range(layers)):
        (low, far, query, key, value, seg_k, reach, context, first_normal, first_inverse,
         normed_low, acts, slopes, second_normal, second_inverse, swapped) = saved[l]
        q_w, k_w, v_w, o_w = head_w[l]
        inner_w, outer_w = unit_w[l, "i"], unit_w[l, "u"]
        grad_mixed, d_second_gain, d_second_shift = norm_back(
            grad_hidden, second_normal, second_inverse, second_gain[l]
        )
        mixed_low = grad_mixed.astype(BF)
        d_outer_bias = jnp.sum(grad_mixed, axis=0)
        mixed_both = mixed_low, g.core(mixed_low)
        normed_both = normed_low, swapped[0]
        outer_parts = unit_parts(acts[: g.nx], swapped[1:], mixed_both)
        outer_parts, mixed_low, grad_mixed, units_before = together(
            outer_parts, mixed_low, grad_mixed, units_before
        )
        if units_before is not None:
            later_sums[l + 1] = over_tensor(units_before)
        if l:
            later_outer[l] = over_tensor([a.reshape(g.nt, block, width) for a in outer_parts])
            outer_sum = None
        else:
            outer_sum = sum_over_x(outer_parts).reshape(g.nt, block, width)
        total, d_inner_bias, grad_inner = feed_forward_back(mixed_low, inner_w, outer_w, slopes)
        inner_parts = unit_parts(grad_inner[: g.nx], [g.core(a) for a in grad_inner[g.nx :]], normed_both)
        grad_normed = grad_mixed + total
        grad_attended, d_first_gain, d_first_shift = norm_back(
            grad_normed, first_normal, first_inverse, first_gain[l]
        )
        inner_parts, grad_attended = together(inner_parts, grad_attended)
        inner_sum = sum_over_x(inner_parts).reshape(g.nt, block, width)
        d_out_bias = jnp.sum(grad_attended, axis=0)
        attended_low = grad_attended.astype(BF)
        grad_context = [dot_nt(attended_low, w).astype(BF) for w in o_w]
        out_total = head_total(context, attended_low)
        backs = []
        for k in range(cores):
            backs.append(attend_back(query[k], key[k], value[k], grad_context[k], seg_q, seg_k, reach))
            if k == 0:
                backs, outer_sum, grad_context, out_total = together(backs, outer_sum, grad_context, out_total)
            elif l == 0:
                outer_sum, out_total = one_step(outer_sum, first_bits[0]), one_step(out_total, first_bits[0])
        backs, outer_sum, out_total = together(backs, outer_sum, out_total)
        d_query, d_key, d_value = zip(*backs)
        far_part = sum(
            dot_nn(a, w) for grad, weight in ((d_key, k_w), (d_value, v_w)) for a, w in zip(grad, weight)
        ).astype(BF)
        near_sum = grad_attended
        for a, w in zip(d_query, q_w):
            near_sum = near_sum + dot_nn(a, w)
        v_total = head_total(d_value, far)
        totals = [head_total(d_query, low), head_total(d_key, far), v_total]
        unit_order = d_inner_bias.reshape(2, g.nx, g.nt, block)
        unit_order = g.turned(g.turned(unit_order, "c", 0), "x", 1)
        if l == 0:
            unit_order = from_steps(unit_order, 2)
        head_grad = jnp.stack(
            [jnp.stack([jnp.sum(a, axis=0, dtype=F32) for a in grad]) for grad in (d_query, d_value)]
        ).reshape(2, cores, g.nt, part)
        if cores == 2:
            head_grad = g.turned(head_grad, "c", 1)
        if l == 0:
            head_grad = from_steps(head_grad, 2)
        vectors[l] = jnp.concatenate(
            [d_out_bias, d_first_gain, d_first_shift, d_outer_bias, d_second_gain, d_second_shift,
             jnp.transpose(unit_order, (2, 1, 0, 3)).reshape(-1),
             jnp.transpose(head_grad, (0, 2, 1, 3)).reshape(-1)]
        )
        if l:
            far_sum = near_sums(far_part) if reach else far_sums(far_part)
            grad_hidden = near_sum + far_sum
            units_before = [inner_sum, *totals, out_total]
    steps_done = cores - 1
    vector = jnp.stack(vectors)
    hops = [(axis, 1 << k) for axis, count in (("dp", g.nd), ("tensor", g.nt)) for k in range(count.bit_length() - 1)]
    far_bits = [1 << k for k in range(group.bit_length() - 1)][::-1]

    def next_hop(vector):
        return vector + g.swap(vector, *hops.pop(0)) if hops else vector

    for bit in first_bits[steps_done : steps_done + 1]:
        outer_sum, out_total = one_step(outer_sum, bit), one_step(out_total, bit)
    inner_sum, totals[2] = one_step(inner_sum, first_bits[0]), one_step(totals[2], first_bits[0])
    vector = next_hop(vector)
    totals, outer_sum, out_total, inner_sum, vector, far_part = together(
        totals, outer_sum, out_total, inner_sum, vector, far_part
    )
    for number, bit in enumerate(first_bits):
        totals[:2] = [one_step(a, bit) for a in totals[:2]]
        if number + 1 < len(first_bits):
            inner_sum = one_step(inner_sum, first_bits[number + 1])
            totals[2] = one_step(totals[2], first_bits[number + 1])
        if number + steps_done + 1 < len(first_bits):
            more = first_bits[number + steps_done + 1]
            outer_sum, out_total = one_step(outer_sum, more), one_step(out_total, more)
        vector = next_hop(vector)
        if far_bits:
            keep, give = jnp.split(far_part, 2)
            far_part = keep.astype(F32) + g.swap(give.astype(BF), "tensor", far_bits.pop(0)).astype(F32)
        if number == 1:
            for l in range(1, layers):
                plain = g.turned(later_outer[l].reshape(-1, block, width), "x", 0).reshape(-1, width)
                ends[l] = end_over_x(later_sums[l][:block], plain, later_sums[l][block:])
        if number == 2:
            for l in range(1, layers):
                ends[l] = end_over_core(*ends[l])
        totals, outer_sum, out_total, inner_sum, vector, far_part, ends = together(
            totals, outer_sum, out_total, inner_sum, vector, far_part, ends
        )
    while far_bits:
        keep, give = jnp.split(far_part, 2)
        far_part = keep.astype(F32) + g.swap(give.astype(BF), "tensor", far_bits.pop(0)).astype(F32)
    grad_hidden = near_sum + far_part
    wide = jnp.concatenate([a.reshape(-1, width) for a in (inner_sum, outer_sum)])
    total = jnp.concatenate([a.reshape(-1, width) for a in (*totals, out_total)])
    vector = next_hop(vector)
    wide, _, total = end_over_x(wide, None, total)
    wide, total, vector = together(wide, total, vector)
    ends[0] = end_over_core(wide, None, total)
    while hops:
        vector = next_hop(vector)

    shared = [vector[:, k * width : (k + 1) * width] for k in range(6)]

    def own_part(start, count):
        return lax.dynamic_slice(vector, (0, start + g.tensor * count), (layers, count))

    d_inner_bias = own_part(6 * width, units)
    d_query_bias = own_part(6 * width + units * g.nt, heads)
    d_value_bias = own_part(6 * width + (units + heads) * g.nt, heads)

    def shard(l, kind):
        wide, plain, total = ends[l]
        if kind == "u" and plain is not None:
            array = plain.reshape(units, width)
        elif kind in "iu":
            k = "iu".index(kind)
            array = wide[:, :, k * block : (k + 1) * block].reshape(units, width)
        else:
            k = "qkvo".index(kind)
            array = total[:, k * part : (k + 1) * part].reshape(heads, width)
        return array

    kinds = [[shard(l, kind) for l in range(layers)] for kind in "qkviou"]
    d_query, d_key, d_value, d_inner, d_out, d_outer = gradients_out(kinds[:4], kinds[4:])
    return (
        result,
        grad_hidden,
        d_query,
        d_query_bias,
        d_key,
        d_value,
        d_value_bias,
        d_out,
        shared[0],
        shared[1],
        shared[2],
        d_inner,
        d_inner_bias,
        d_outer,
        shared[3],
        shared[4],
        shared[5],
    )


def solution(mesh):
    rows = P(("dp", "tensor"), None)
    columns = P(None, None, "tensor")
    units = P(None, "tensor", None)
    vector = P(None, "tensor")
    in_specs = (
        rows, P("dp", None), columns, vector, columns, columns, vector, units, P(), P(), P(),
        columns, vector, units, P(), P(), P(), rows,
    )
    out_specs = (
        rows, rows, columns, vector, columns, columns, vector, units, P(), P(), P(),
        columns, vector, units, P(), P(), P(),
    )
    return jax.shard_map(
        partial(shards, Grid(mesh)), mesh=mesh, in_specs=in_specs, out_specs=out_specs, check_vma=False
    )
```
